128 devices in a mesh: gz: 8 (over x, z_hi), ta: 16 (over y, z_lo, core).
Axes of the slice: x: 4, y: 4, z: 4 (z_hi: 2, z_lo: 2; z = z_hi * 2 + z_lo), core: 2. Of those that a mesh axis runs over, the one named last changes fastest.
Arguments:
- source: float32 [24, 32, 128, 128], P(None, 'gz', 'ta'), may hold values from -6 to 6
- gauge_links: float32 [4, 18, 32, 128, 128], P(None, None, 'gz', 'ta'), may hold values from -2.5 to 2.5
- clover_term: float32 [2, 2, 6, 6, 32, 128, 128], P(None, None, None, None, 'gz', 'ta'), may hold values from -0.9 to 0.9
- null_vectors: bfloat16 [24, 24, 32, 128, 128], P(None, None, 'gz', 'ta'), may hold values from -0.109375 to 0.109375
- owners: int32 [2048, 1], P(('gz', 'ta')), may hold values from 0 to 15; in each aligned block of 16 rows (0 to 15, 16 to 31, ...) at most 2 rows name the same one
Outputs:
- solution: float32 [24, 32, 128, 128], P(None, 'gz', 'ta')
- coarse: float32 [96, 4096], P(None, ('gz', 'ta'))
The draws below stay inside these ranges and needn't reach their ends.
Inputs may be any that keep to these rules, and one draw needn't show every extreme that they name: `owners`: in each aligned block of 16 rows no owner is named more than 2 times, and in some block one owner is named exactly that often.
All inputs are finite; a program needn't handle non-finite values.
Results may differ from the reference program's by a relative error of at most 0.0029.
Values sent between devices are 32-bit elements; how exact they have to be, the bound alone decides.
A program may use at most 128 MiB of HBM per device.

```python
import math
import jax
import jax.numpy as jnp
import numpy as np
from jax import lax

LX = 8
LY = 16
ZDEV = 4
AGG = 4
NVEC = 24
SWEEPS = 4
NZ = 32
NT = 128
XY = 128
AGG_SITES = 256
AGG_DEV = 16
AGGS = 2048
SEND_MOST = 2
COARSE_COLS = 4096
N_GZ = 8
N_TA = 16


def level_of(stream_key, dims, shards, low, high):
    def one(axis_at, shards_of):
        draws = jax.random.uniform(jax.random.fold_in(jax.random.fold_in(stream_key, 6), axis_at), (shards_of,), jnp.float32, low / len(shards), high / len(shards))
        return jnp.repeat(jnp.exp(draws), dims[axis_at] // shards_of).reshape((-1,) + (1,) * (len(dims) - axis_at - 1))

    level = one(*shards[0])
    for cut in shards[1:]:
        level = level * one(*cut)
    return level


def routed_block(stream_key, own, number, rows, number_of, top, limit, slope):
    ranking = jax.random.permutation(stream_key, number_of)
    heavy_load, common = shares(number_of, rows * top, limit, slope, True), shares(number_of, rows * top, limit, slope, False)
    places = jnp.arange(number_of)

    def named(lengths, turn):
        used = int((lengths > 0).sum())
        fixed = max(1, used // 4)
        moved = fixed + (places - fixed + turn * (used - fixed)) % max(1, number_of - fixed)
        return jnp.zeros((number_of,), jnp.int32).at[ranking[jnp.where(places < fixed, places, moved)]].set(jnp.asarray(lengths, jnp.int32))

    lengths = jnp.where(number % 4 == 0, named(heavy_load, number // 4), named(common, number - number // 4 - 1))
    mixed = jax.random.permutation(jax.random.fold_in(own, 3), number_of)
    giver, receiver = mixed[0:number_of // 2 * 2:2], mixed[1:number_of // 2 * 2:2]
    margin = jnp.minimum(lengths[giver] - 1, limit - lengths[receiver]) // 2
    margin = jnp.where((giver == ranking[0]) | (receiver == ranking[0]) | (lengths[receiver] == 0), 0, jnp.maximum(margin, 0))
    moved = jax.random.randint(jax.random.fold_in(own, 4), (number_of // 2,), 0, 1 << 20) % (margin + 1)
    lengths = lengths.at[giver].add(-moved).at[receiver].add(moved)
    items = jnp.searchsorted(jnp.cumsum(lengths), jnp.arange(rows * top), side="right").astype(jnp.int32)
    listing = items.reshape(top, rows).T
    listing = listing[jax.random.permutation(jax.random.fold_in(own, 1), rows)]
    turn = jax.random.randint(jax.random.fold_in(own, 2), (rows, 1), 0, top)
    return jnp.take_along_axis(listing, (jnp.arange(top)[None, :] + turn) % top, axis=1)


def shares(number_of, total, limit, skew, full):
    weights = [(1 << 20) // math.isqrt(standing ** skew) + 1 for standing in range(1, number_of + 1)]
    largest = limit if full else min(limit, max(-(-total // number_of), total * weights[0] // sum(weights)))
    least = 1 if total - largest >= number_of - 1 else 0
    counts, spare = [largest] + [least] * (number_of - 1), total - largest - least * (number_of - 1)
    while spare > 0:
        candidates = [i for i in range(1, number_of) if counts[i] < largest] or [i for i in range(1, number_of) if counts[i] < limit]
        pool, left = sum([weights[i] for i in candidates]), spare
        for i in candidates:
            addition = min(limit - counts[i], max(1, left * weights[i] // pool), spare)
            counts[i] = counts[i] + addition
            spare = spare - addition
    return np.array(counts)


def bell_draw(key, dims, width, limit, pieces=(), kind=jnp.bfloat16):
    values = width * jax.random.normal(key, dims, jnp.float32)
    if pieces:
        values = values * level_of(key, dims, pieces, -0.22, 0.18)
    return jnp.clip(values, -limit, limit).astype(kind)


def setup_inputs(seed: int = 0) -> dict:
    splits = jax.random.split(jax.random.key(seed), 6)
    source = bell_draw(splits[0], (24, NZ, NT, XY), 1.0, 6.0, ((1, 8), (2, 16)), jnp.float32)
    gauge_links = bell_draw(splits[1], (4, 18, NZ, NT, XY), 6 ** -0.5, 2.5, ((2, 8), (3, 16)), jnp.float32)
    clover_term = bell_draw(splits[2], (2, 2, 6, 6, NZ, NT, XY), 0.15, 0.9, ((4, 8), (5, 16)), jnp.float32)
    null_vectors = bell_draw(splits[3], (NVEC, 24, NZ, NT, XY), (12 * AGG_SITES) ** -0.5, 0.109375, ((2, 8), (3, 16)))
    owners_keys = jax.random.split(jax.random.fold_in(splits[4], 1), AGGS // AGG_DEV)
    owners_turns = jax.random.permutation(jax.random.fold_in(splits[4], 3), AGGS // AGG_DEV)
    owners = jax.vmap(lambda own, number: routed_block(jax.random.fold_in(splits[4], 2), own, number, AGG_DEV, N_TA, 1, SEND_MOST, 2))(owners_keys, owners_turns).reshape((AGGS, 1))
    return {"source": source, "gauge_links": gauge_links, "clover_term": clover_term, "null_vectors": null_vectors, "owners": owners}


mass_diagonal = 4.2
relax_weight = 0.24
full_precision = lax.Precision.HIGHEST


def gamma_matrix(direction):
    paulis = [np.array([[0, 1], [1, 0]], dtype=complex), np.array([[0, -1j], [1j, 0]], dtype=complex), np.array([[1, 0], [0, -1]], dtype=complex)]
    result = np.zeros((4, 4), dtype=complex)
    if direction < 3:
        result[:2, 2:] = -1j * paulis[direction]
        result[2:, :2] = 1j * paulis[direction]
    else:
        result[:2, 2:] = np.eye(2)
        result[2:, :2] = np.eye(2)
    return result


def real_block(matrix):
    rows_half = matrix.shape[0]
    cols_half = matrix.shape[1]
    result = np.zeros((2 * rows_half, 2 * cols_half))
    result[:rows_half, :cols_half] = matrix.real
    result[:rows_half, cols_half:] = -matrix.imag
    result[rows_half:, :cols_half] = matrix.imag
    result[rows_half:, cols_half:] = matrix.real
    return result


def projector(direction, parity):
    return np.eye(4) + parity * gamma_matrix(direction)


def spin_apply(matrix, spinor):
    row_count = matrix.shape[0]
    flattened = spinor.reshape((spinor.shape[0] * spinor.shape[1],) + spinor.shape[2:])
    product = jnp.einsum("ab,bcztx->acztx", jnp.asarray(matrix, jnp.float32), flattened, precision=full_precision)
    return product.reshape((2, row_count // 2) + spinor.shape[2:])


def colour_apply(link_field, spinor, dagger):
    site_shape = link_field.shape[1:]
    real_link = link_field[:9].reshape((3, 3) + site_shape)
    imag_link = link_field[9:].reshape((3, 3) + site_shape)
    pattern = "baztx,pbztx->paztx" if dagger else "abztx,pbztx->paztx"

    def multiply(matrix, vector):
        return jnp.einsum(pattern, matrix, vector, precision=full_precision)

    real_in, imag_in = spinor[0], spinor[1]
    if dagger:
        real_out = multiply(real_link, real_in) + multiply(imag_link, imag_in)
        imag_out = multiply(real_link, imag_in) - multiply(imag_link, real_in)
    else:
        real_out = multiply(real_link, real_in) - multiply(imag_link, imag_in)
        imag_out = multiply(real_link, imag_in) + multiply(imag_link, real_in)
    return jnp.stack([real_out, imag_out])


def clover_apply(clover_term, spinor):
    site_shape = spinor.shape[3:]
    halves = spinor.reshape((2, 2, 6) + site_shape)
    clover_real = clover_term[:, 0]
    clover_imag = clover_term[:, 1]

    def multiply(matrix, vector):
        return jnp.einsum("habztx,hbztx->haztx", matrix, vector, precision=full_precision)

    real_out = multiply(clover_real, halves[0]) - multiply(clover_imag, halves[1])
    imag_out = multiply(clover_real, halves[1]) + multiply(clover_imag, halves[0])
    return jnp.stack([real_out, imag_out]).reshape(spinor.shape)


def neighbour(spinor, direction, step_sign):
    if direction == 0:
        return jnp.roll(spinor, -step_sign * LY, axis=-1)
    if direction == 1:
        y_coord = lax.broadcasted_iota(jnp.int32, (spinor.shape[-1],), 0) % LY
        if step_sign == 1:
            return jnp.where(y_coord == LY - 1, jnp.roll(spinor, LY - 1, axis=-1), jnp.roll(spinor, -1, axis=-1))
        return jnp.where(y_coord == 0, jnp.roll(spinor, -(LY - 1), axis=-1), jnp.roll(spinor, 1, axis=-1))
    if direction == 2:
        return jnp.roll(spinor, -step_sign, axis=3)
    moved = jnp.roll(spinor, -step_sign, axis=4)
    t_coord = lax.broadcasted_iota(jnp.int32, (spinor.shape[4], 1), 0)
    edge_index = spinor.shape[4] - 1 if step_sign == 1 else 0
    return jnp.where(t_coord == edge_index, -moved, moved)


def dirac_apply(vector_field, gauge_links, clover_term):
    spinor = vector_field.reshape((2, 4, 3) + vector_field.shape[1:])
    hopping = None
    for direction in range(4):
        forward = colour_apply(gauge_links[direction], spin_apply(real_block(projector(direction, -1.0)), neighbour(spinor, direction, 1)), False)
        backward = neighbour(colour_apply(gauge_links[direction], spin_apply(real_block(projector(direction, 1.0)), spinor), True), direction, -1)
        hop_term = forward + backward
        hopping = hop_term if hopping is None else hopping + hop_term
    result = mass_diagonal * spinor + clover_apply(clover_term, spinor) - 0.5 * hopping
    return result.reshape(vector_field.shape)


def aggregate_values(resid_slab, vector_slab, t_groups):
    site_shape = resid_slab.shape[1:]
    vector_count = vector_slab.shape[0]
    real_resid = resid_slab[:12].reshape((2, 6) + site_shape)
    imag_resid = resid_slab[12:].reshape((2, 6) + site_shape)
    real_vec = vector_slab[:, :12].reshape((vector_count, 2, 6) + site_shape)
    imag_vec = vector_slab[:, 12:].reshape((vector_count, 2, 6) + site_shape)

    def contract(left_side, right_side):
        return jnp.einsum("vhcztx,hcztx->vhztx", left_side, right_side, precision=full_precision)

    real_part = contract(real_vec, real_resid) + contract(imag_vec, imag_resid)
    imag_part = contract(real_vec, imag_resid) - contract(imag_vec, real_resid)
    stacked = jnp.stack([real_part, imag_part])
    z_count = site_shape[0]
    t_count = site_shape[1]
    blocks = stacked.reshape((2, vector_count, 2, z_count // AGG, AGG, t_groups, t_count // (t_groups * AGG), AGG, LX // AGG, AGG, LY // AGG, AGG))
    summed = blocks.sum(axis=(4, 7, 9, 11))
    ordered = summed.transpose((4, 0, 2, 1, 3, 5, 6, 7))
    return ordered.reshape((t_groups, 4 * vector_count, -1))


def reference(source, gauge_links, clover_term, null_vectors, owners):
    solution = relax_weight * source
    for sweep_index in range(SWEEPS - 1):
        solution = solution + relax_weight * (source - dirac_apply(solution, gauge_links, clover_term))
    residual = (source - dirac_apply(solution, gauge_links, clover_term)).astype(jnp.bfloat16)

    def restrict_slab(slab_index):
        start = (slab_index * ZDEV).astype(jnp.int32)
        resid_slab = lax.dynamic_slice_in_dim(residual, start, ZDEV, axis=1).astype(jnp.float32)
        vector_slab = lax.dynamic_slice_in_dim(null_vectors, start, ZDEV, axis=2).astype(jnp.float32)
        return aggregate_values(resid_slab, vector_slab, N_TA)

    slabs = lax.map(restrict_slab, jnp.arange(N_GZ, dtype=jnp.int32))
    devices_total = N_GZ * N_TA
    values = slabs.reshape((devices_total, 4 * NVEC, AGG_DEV))
    owner_index = owners[:, 0].reshape((devices_total, AGG_DEV)).astype(jnp.int32)
    later_index = lax.broadcasted_iota(jnp.int32, (AGG_DEV, AGG_DEV), 0)
    other_index = lax.broadcasted_iota(jnp.int32, (AGG_DEV, AGG_DEV), 1)
    same_owner = owner_index[:, :, None] == owner_index[:, None, :]
    earlier = jnp.sum((same_owner & (other_index < later_index)[None]).astype(jnp.int32), axis=2)
    device_index = lax.broadcasted_iota(jnp.int32, (devices_total, AGG_DEV), 0)
    slab_z = device_index // N_TA
    slab_t = device_index % N_TA
    column = ((slab_z * N_TA + owner_index) * N_TA + slab_t) * SEND_MOST + earlier
    placed = values.transpose((1, 0, 2)).reshape((4 * NVEC, devices_total * AGG_DEV))
    coarse = jnp.zeros((4 * NVEC, COARSE_COLS), jnp.float32).at[:, column.reshape(-1).astype(jnp.int32)].set(placed)
    return solution, coarse
```

```python
import jax
import jax.numpy as jnp
from jax import lax
from jax.experimental import pallas as pl
from jax.experimental.pallas import tpu as pltpu
from jax.sharding import PartitionSpec as P

MESH = pl.DeviceIdType.MESH
F32 = jnp.float32
BF16 = jnp.bfloat16

NZ = 4
COMPS = 24
VECS = 24
GZ = 8
TA = 16
PLANE = 32
FIELD = COMPS * PLANE
WEIGHT = 0.24
MASS = 4.2
HALF = 0.5 * WEIGHT
KAPPA = 2.0 / WEIGHT - 2.0 * MASS
X, Y, Z, T = 0, 1, 2, 3

SPIN = {
    X: [[(-1, 1, 1), (-1, 1, 0)], [(1, 0, 1), (1, 0, 0)]],
    Y: [[(1, 0, 1), (-1, 0, 0)], [(1, 1, 1), (-1, 1, 0)]],
    Z: [[(-1, 1, 0), (1, 1, 1)], [(1, 0, 0), (-1, 0, 1)]],
    T: [[(-1, 0, 0), (-1, 0, 1)], [(-1, 1, 0), (-1, 1, 1)]],
}
INVERSE = {X: -1, Y: -1, Z: -1, T: 1}


def comp(reim, spin, colour):
    return 12 * reim + 3 * spin + colour


def half(reim, spin, colour):
    return 6 * reim + 3 * spin + colour


def add(a, b, sign):
    return a + b if sign > 0 else a - b


def project(load, direction, parity, s):
    out = []
    for r in range(2):
        sign, r2, s2 = SPIN[direction][r][s]
        out.append([add(load(r, s, c), load(r2, 2 + s2, c), -parity * sign) for c in range(3)])
    return out


def colour(link, a, dagger):
    re, im = [], []
    for row in range(3):
        tr = ti = None
        for k in range(3):
            e = 3 * k + row if dagger else 3 * row + k
            lr, li = link[e], link[9 + e]
            if dagger:
                nr = lr * a[0][k] + li * a[1][k]
                ni = lr * a[1][k] - li * a[0][k]
            else:
                nr = lr * a[0][k] - li * a[1][k]
                ni = lr * a[1][k] + li * a[0][k]
            tr = nr if tr is None else tr + nr
            ti = ni if ti is None else ti + ni
        re.append(tr)
        im.append(ti)
    return [re, im]


def lower_terms(direction, s):
    out = []
    for r in range(2):
        for spin in range(2):
            sign, r2, s2 = SPIN[direction][r][spin]
            if s2 == s:
                out.append((INVERSE[direction] * sign, r2, r, 2 + spin))
    return out


def kernel(
    source, links, clover, vectors, owners, x_out, coarse_out,
    y, g, cl, v, sz, st, sr, sl, rz, rt, rd, rl, tmp, wt, place, so, rc, xs,
    load_sem, msg_send, msg_recv, diag_send, diag_recv, link_send, link_recv, all_send, all_recv, x_sem,
):
    me_z = lax.axis_index("gz")
    me_t = lax.axis_index("ta")

    def device(dz, dt):
        return (lax.rem(me_z + (dz + GZ), GZ), lax.rem(me_t + (dt + TA), TA))

    loads = [
        pltpu.make_async_copy(source, y.at[pl.ds(0, FIELD)], load_sem.at[0]),
        pltpu.make_async_copy(links, g, load_sem.at[1]),
        pltpu.make_async_copy(clover, cl, load_sem.at[2]),
        pltpu.make_async_copy(vectors, v, load_sem.at[3]),
    ]
    for c in loads:
        c.start()

    barrier = pltpu.get_barrier_semaphore()
    greet = [(dz, dt) for dz in (-1, 1) for dt in (-1, 0, 1)] + [(0, dt) for dt in range(1, TA)]
    for dz, dt in greet:
        pl.semaphore_signal(barrier, inc=1, device_id=device(dz, dt), device_id_type=MESH)

    down_sign = jnp.where(me_t == 0, -1.0, 1.0).astype(F32)
    up_sign = jnp.where(me_t == TA - 1, -1.0, 1.0).astype(F32)

    sub = lax.broadcasted_iota(jnp.int32, (16, 128), 0)
    lane = lax.broadcasted_iota(jnp.int32, (16, 128), 1)
    own = jnp.broadcast_to(owners[...].astype(F32), (16, 128))
    own_row = jnp.sum(jnp.where(sub == lane, own, 0.0), axis=0, keepdims=True)
    rank = jnp.sum(jnp.where((own == own_row) & (lane < sub), 1.0, 0.0), axis=1, keepdims=True)
    slot = own * 8.0 + rank
    for part in range(2):
        agg = ((lane & 7) >> 2) * 8 + ((lane >> 4) & 7)
        of_lane = jnp.sum(jnp.where(agg == sub, slot, 0.0), axis=0, keepdims=True)
        row = lax.broadcasted_iota(jnp.int32, (128, 128), 0).astype(F32)
        place[:, 128 * part:128 * (part + 1)] = jnp.where(row == of_lane, 1.0, 0.0)

    for j in (0, 2, 4, 6, 8, 9, 12, 13):
        for e in (0, 8, 16):
            diag = lax.broadcasted_iota(jnp.int32, (8, 128), 0) + e
            rl[pl.ds(24 * j + e, 8), :] = jnp.where(
                (diag == 0) | (diag == 4) | (diag == 8), jnp.ones((8, 128), F32), 0.0
            )

    def yrow(k, c, z, t=0):
        return k * FIELD + c * PLANE + z * 8 + t

    def y_at(k, z):
        def load(r, s, c):
            return y[pl.ds(pl.multiple_of(yrow(k, comp(r, s, c), z), 8), 8), :]
        return load

    def link_at(direction, z):
        return [
            g[pl.ds(pl.multiple_of((18 * direction + e) * PLANE + z * 8, 8), 8), :]
            for e in range(18)
        ]

    def bump(k, z, r, s, c, value, sign=1):
        at = pl.ds(pl.multiple_of(yrow(k, comp(r, s, c), z), 8), 8)
        y[at, :] = add(y[at, :], value, sign)

    y_lane = lax.broadcasted_iota(jnp.int32, (8, 128), 1) & 15
    t_row = lax.broadcasted_iota(jnp.int32, (8, 128), 0)

    def ahead(direction, a):
        if direction == X:
            return pltpu.roll(a, 112, 1)
        if direction == Y:
            return jnp.where(y_lane == 15, pltpu.roll(a, 15, 1), pltpu.roll(a, 127, 1))
        return jnp.where(t_row == 7, 0.0, pltpu.roll(a, 7, 0))

    def behind(direction, a):
        if direction == X:
            return pltpu.roll(a, 16, 1)
        if direction == Y:
            return jnp.where(y_lane == 0, pltpu.roll(a, 113, 1), pltpu.roll(a, 1, 1))
        return jnp.where(t_row == 0, 0.0, pltpu.roll(a, 1, 0))

    def layer(k, z):
        load = y_at(k, z)
        for h in range(2):
            vr = [load(0, 2 * h + i // 3, i % 3) for i in range(6)]
            vi = [load(1, 2 * h + i // 3, i % 3) for i in range(6)]
            ur = [-2.0 * a for a in vr]
            ui = [-2.0 * a for a in vi]
            for row in range(6):
                tr = KAPPA * vr[row]
                ti = KAPPA * vi[row]
                for k2 in range(6):
                    base = ((2 * h) * 6 + row) * 6 + k2
                    cr = cl[pl.ds(pl.multiple_of(base * PLANE + z * 8, 8), 8), :]
                    ci = cl[pl.ds(pl.multiple_of((base + 36) * PLANE + z * 8, 8), 8), :]
                    tr = tr + (cr * ur[k2] - ci * ui[k2])
                    ti = ti + (cr * ui[k2] + ci * ur[k2])
                s, c = 2 * h + row // 3, row % 3
                y[pl.ds(pl.multiple_of(yrow(k + 1, comp(0, s, c), z), 8), 8), :] = tr
                y[pl.ds(pl.multiple_of(yrow(k + 1, comp(1, s, c), z), 8), 8), :] = ti
        for direction in (X, Y, T):
            link = link_at(direction, z)
            for s in range(2):
                fwd = project(load, direction, -1, s)
                fwd = [[ahead(direction, a) for a in part] for part in fwd]
                fwd = colour(link, fwd, False)
                bwd = colour(link, project(load, direction, 1, s), True)
                bwd = [[behind(direction, a) for a in part] for part in bwd]
                for r in range(2):
                    for c in range(3):
                        bump(k + 1, z, r, s, c, fwd[r][c] + bwd[r][c])
                for sign, r2, r, s2 in lower_terms(direction, s):
                    for c in range(3):
                        bump(k + 1, z, r, s2, c, fwd[r2][c] - bwd[r2][c], sign)

    def z_link(k, z):
        link = link_at(Z, z)
        for s in range(2):
            fwd = colour(link, project(y_at(k, z + 1), Z, -1, s), False)
            put_half(k + 1, z, s, fwd, 1)
            bwd = colour(link, project(y_at(k, z), Z, 1, s), True)
            put_half(k + 1, z + 1, s, bwd, -1)

    def put_half(k, z, s, w, parity):
        for r in range(2):
            for c in range(3):
                bump(k, z, r, s, c, w[r][c])
        for sign, r2, r, s2 in lower_terms(Z, s):
            for c in range(3):
                bump(k, z, r, s2, c, w[r2][c], parity * sign)

    def local(k, at_third):
        def step(i, carry):
            z = lax.rem(i + 1, NZ)
            if at_third is not None:
                @pl.when(i == 2)
                def _():
                    at_third()
            layer(k, z)

            @pl.when(i > 0)
            def _():
                z_link(k, lax.rem(i, 3))
            return carry
        lax.fori_loop(0, NZ, step, 0)

    def rows_of(k, t):
        def load(r, s, c):
            return y[pl.ds(yrow(k, comp(r, s, c), 0, t), NZ, stride=8), :]
        return load

    def link_rows(t):
        return [g[pl.ds((18 * T + e) * PLANE + t, NZ, stride=8), :] for e in range(18)]

    def pack(k):
        link = link_at(Z, NZ - 1)
        tlink = link_rows(7)
        for s in range(2):
            dn = project(y_at(k, 0), Z, -1, s)
            up = colour(link, project(y_at(k, NZ - 1), Z, 1, s), True)
            for r in range(2):
                for c in range(3):
                    sz[k, 0, pl.ds(8 * half(r, s, c), 8), :] = dn[r][c]
                    sz[k, 1, pl.ds(8 * half(r, s, c), 8), :] = up[r][c]
            dn = project(rows_of(k, 0), T, -1, s)
            up = colour(tlink, project(rows_of(k, 7), T, 1, s), True)
            for r in range(2):
                for c in range(3):
                    at = pl.ds(8 * r + 3 * s + c, NZ, stride=16)
                    st[k, 0, at, :] = dn[r][c] * down_sign
                    st[k, 1, at, :] = up[r][c] * up_sign

    def pack_corners(p, k):
        for m in range(2):
            for i, (t, sign) in enumerate(((0, down_sign), (7, up_sign))):
                for r in range(2):
                    rows = sz[k, m, pl.ds(48 * r + t, 6, stride=8), :]
                    sr[p, 2 * m + i, pl.ds(8 * r, 6), :] = rows * sign

    def message(k, m):
        target = ((-1, 0), (1, 0), (0, -1), (0, 1))[m]
        src, dst = (sz, rz) if m < 2 else (st, rt)
        return pltpu.make_async_remote_copy(
            src_ref=src.at[k, m % 2], dst_ref=dst.at[k, m % 2],
            send_sem=msg_send.at[k, m], recv_sem=msg_recv.at[k, m],
            device_id=device(*target), device_id_type=MESH,
        )

    def corner(p, k, j):
        src = (
            st.at[k, 1, pl.ds(0, 16)], st.at[k, 0, pl.ds(0, 16)],
            st.at[k, 1, pl.ds(48, 16)], st.at[k, 0, pl.ds(48, 16)],
            sr.at[p, 2], sr.at[p, 0], sr.at[p, 3], sr.at[p, 1],
        )[j]
        target = ((-1, 1), (-1, -1), (1, 1), (1, -1), (1, -1), (-1, -1), (1, 1), (-1, 1))[j]
        return pltpu.make_async_remote_copy(
            src_ref=src, dst_ref=rd.at[p, pl.ds(16 * j, 16)],
            send_sem=diag_send.at[p, j], recv_sem=diag_recv.at[p, j],
            device_id=device(*target), device_id_type=MESH,
        )

    def corner_link(i):
        block, target, to = (
            (0, (-1, 0), 1), (1, (1, 0), 3), (2, (1, 0), 10), (3, (1, 0), 11),
            (2, (0, -1), 5), (3, (0, 1), 7), (0, (0, 1), 14), (1, (0, 1), 15),
        )[i]
        return pltpu.make_async_remote_copy(
            src_ref=sl.at[block], dst_ref=rl.at[pl.ds(24 * to, 24)],
            send_sem=link_send.at[i], recv_sem=link_recv.at[i],
            device_id=device(*target), device_id_type=MESH,
        )

    def finish_t(k):
        link = link_rows(7)
        for s in range(2):
            a = [[rt[k, 0, pl.ds(8 * r + 3 * s + c, NZ, stride=16), :] for c in range(3)] for r in range(2)]
            b = [[rt[k, 1, pl.ds(8 * r + 3 * s + c, NZ, stride=16), :] for c in range(3)] for r in range(2)]
            for w, t, parity in ((colour(link, a, False), 7, 1), (b, 0, -1)):
                def bump_row(r, s, c, value, sign):
                    at = pl.ds(yrow(k + 1, comp(r, s, c), 0, t), NZ, stride=8)
                    y[at, :] = add(y[at, :], value, sign)
                for r in range(2):
                    for c in range(3):
                        bump_row(r, s, c, w[r][c], 1)
                for sign, r2, r, s2 in lower_terms(T, s):
                    for c in range(3):
                        bump_row(r, s2, c, w[r2][c], parity * sign)

    def finish_z(k):
        link = link_at(Z, NZ - 1)
        for s in range(2):
            a = [[rz[k, 0, pl.ds(8 * half(r, s, c), 8), :] for c in range(3)] for r in range(2)]
            put_half(k + 1, NZ - 1, s, colour(link, a, False), 1)
            b = [[rz[k, 1, pl.ds(8 * half(r, s, c), 8), :] for c in range(3)] for r in range(2)]
            put_half(k + 1, 0, s, b, -1)

    def correct(p, k):
        one = [rl[pl.ds(e, 8, stride=24), :] for e in range(18)]
        two = [rl[pl.ds(192 + e, 8, stride=24), :] for e in range(18)]
        j = lax.broadcasted_iota(jnp.int32, (8, 128), 0)
        plus = (j == 0) | (j == 3) | (j == 5) | (j == 6)
        sign_j = jnp.where(plus, jnp.ones((8, 128), F32), -1.0)
        w = []
        for s in range(2):
            a = [[rd[p, pl.ds(8 * r + 3 * s + c, 8, stride=16), :] for c in range(3)] for r in range(2)]
            w.append(colour(one, a, False))
        for s in range(2):
            q = []
            for r in range(2):
                sign, r2, s2 = SPIN[Z][r][s]
                q.append([add(w[s][r][c], sign_j * w[s2][r2][c], sign) for c in range(3)])
            q = colour(two, q, True)
            for r in range(2):
                for c in range(3):
                    tmp[pl.ds(8 * half(r, s, c), 8), :] = q[r][c]
        for s in range(2):
            for r in range(2):
                for c in range(3):
                    n = half(r, s, c)
                    for m in range(2):
                        at = pl.ds(8 * n, 2, stride=7)
                        rz[k, m, at, :] = rz[k, m, at, :] + tmp[pl.ds(8 * n + 2 * m, 2), :]
                        at = pl.ds(8 * r + 3 * s + c, 2, stride=48)
                        rt[k, m, at, :] = rt[k, m, at, :] + tmp[pl.ds(8 * n + 4 + 2 * m, 2), :]

    loads[0].wait()
    loads[1].wait()
    for i, (direction, z, t) in enumerate(((T, 0, 7), (T, 3, 7), (Z, 3, 0), (Z, 3, 7))):
        for e, count in ((0, 8), (8, 8), (16, 2)):
            sl[i, pl.ds(e, count), :] = g[pl.ds((18 * direction + e) * PLANE + z * 8 + t, count, stride=32), :]
    loads[2].wait()
    pl.semaphore_wait(barrier, len(greet))

    for p in range(2):
        k = 2 * p
        pack(k)
        for m in range(4):
            message(k, m).start()
        pack_corners(p, k)
        for j in range(8):
            corner(p, k, j).start()
        if p == 0:
            for i in range(8):
                corner_link(i).start()
        local(k, None)
        pack(k + 1)
        for m in range(4):
            message(k + 1, m).start()
        message(k, 2).wait_recv()
        message(k, 3).wait_recv()
        finish_t(k)

        def at_third():
            message(k, 0).wait_recv()
            message(k, 1).wait_recv()
            finish_z(k)
        local(k + 1, at_third)
        for j in range(8):
            corner(p, k, j).wait_recv()
        if p == 0:
            for i in range(8):
                corner_link(i).wait_recv()
        for m in range(4):
            message(k + 1, m).wait_recv()
        correct(p, k + 1)
        finish_t(k + 1)
        finish_z(k + 1)

    loads[3].wait()
    site = lax.broadcasted_iota(jnp.int32, (16, 128), 1)
    group = (site >> 6) * 4 + ((site & 15) >> 2)
    scale = HALF ** 4
    pooled = []
    for h in range(2):
        left = []
        for zp in range(2):
            for c in range(6):
                rows = []
                for r in range(2):
                    n = comp(r, 2 * h, 0) + c
                    rows.append((y[pl.ds(yrow(4, n, 2 * zp), 16), :] * scale).astype(BF16))
                    left.append(v[:, pl.ds(n * PLANE + 16 * zp, 16), :].reshape(VECS * 16, 128))
                col = (zp * 6 + c) * 256
                for grp in range(8):
                    keep = (group == grp).astype(F32).astype(BF16)
                    re, im = rows[0] * keep, rows[1] * keep
                    wt[pl.ds(16 * grp, 16), col:col + 128] = re
                    wt[pl.ds(16 * grp, 16), col + 128:col + 256] = im
                    wt[pl.ds(128 + 16 * grp, 16), col:col + 128] = im
                    wt[pl.ds(128 + 16 * grp, 16), col + 128:col + 256] = -re
        prod = lax.dot_general(
            jnp.concatenate(left, axis=1), wt[...], (((1,), (1,)), ((), ())), preferred_element_type=F32
        )
        i0 = lax.broadcasted_iota(jnp.int32, (VECS * 16, 256), 0) & 15
        i1 = lax.broadcasted_iota(jnp.int32, (VECS * 16, 256), 1) & 15
        prod = jnp.where(i0 == i1, prod, 0.0)
        pooled.append(jnp.sum(prod.reshape(VECS, 16, 256), axis=1))
    zero = jnp.zeros((2 * VECS, 128), F32)
    pooled = jnp.concatenate(pooled, axis=0)
    first = jnp.concatenate([pooled[:, :128], zero], axis=1)
    second = jnp.concatenate([zero, pooled[:, 128:]], axis=1)
    values = jnp.concatenate([first, second, jnp.zeros((32, 256), F32)], axis=0)
    so[...] = lax.dot_general(
        place[...], values, (((1,), (1,)), ((), ())), preferred_element_type=F32,
        precision=lax.Precision.HIGHEST,
    )

    def exchange(d):
        to = lax.rem(me_t + d, TA)
        return pltpu.make_async_remote_copy(
            src_ref=so.at[pl.ds(pl.multiple_of(8 * to, 8), 8)],
            dst_ref=rc.at[pl.ds(pl.multiple_of(8 * me_t, 8), 8)],
            send_sem=all_send.at[d], recv_sem=all_recv.at[d],
            device_id=(me_z, to), device_id_type=MESH,
        )

    for d in range(1, TA):
        exchange(d).start()
    mine = pl.ds(pl.multiple_of(8 * me_t, 8), 8)
    rc[mine, :] = so[mine, :]

    def solution_rows(i, carry):
        at = [pl.ds(pl.multiple_of(n * FIELD + i * 32, 8), 32) for n in range(4)]
        total = y[at[2], :] + HALF * y[at[3], :]
        total = y[at[1], :] + HALF * total
        total = y[at[0], :] + HALF * total
        xs[at[0], :] = WEIGHT * total
        return carry
    lax.fori_loop(0, COMPS, solution_rows, 0)
    write = pltpu.make_async_copy(xs, x_out, x_sem)
    write.start()

    for d in range(1, TA):
        exchange(d).wait()
    coarse_out[...] = rc[...]
    for p in range(2):
        for m in range(4):
            message(2 * p, m).wait_send()
            message(2 * p + 1, m).wait_send()
        for j in range(8):
            corner(p, 2 * p, j).wait_send()
    for i in range(8):
        corner_link(i).wait_send()
    write.wait()


def on_device(source, gauge_links, clover_term, null_vectors, owners):
    any_space = pl.BlockSpec(memory_space=pl.ANY)
    vmem = pl.BlockSpec(memory_space=pltpu.VMEM)
    dma = pltpu.SemaphoreType.DMA
    x, coarse = pl.pallas_call(
        kernel,
        out_shape=(jax.ShapeDtypeStruct((FIELD, 128), F32), jax.ShapeDtypeStruct((128, 128), F32)),
        in_specs=[any_space, any_space, any_space, any_space, vmem],
        out_specs=(any_space, vmem),
        scratch_shapes=[
            pltpu.VMEM((5 * FIELD, 128), F32),
            pltpu.VMEM((72 * PLANE, 128), F32),
            pltpu.VMEM((144 * PLANE, 128), F32),
            pltpu.VMEM((VECS, FIELD, 128), BF16),
            pltpu.VMEM((4, 2, 96, 128), F32),
            pltpu.VMEM((4, 2, 64, 128), F32),
            pltpu.VMEM((2, 4, 16, 128), F32),
            pltpu.VMEM((4, 24, 128), F32),
            pltpu.VMEM((4, 2, 96, 128), F32),
            pltpu.VMEM((4, 2, 64, 128), F32),
            pltpu.VMEM((2, 128, 128), F32),
            pltpu.VMEM((16 * 24, 128), F32),
            pltpu.VMEM((96, 128), F32),
            pltpu.VMEM((256, 3072), BF16),
            pltpu.VMEM((128, 256), F32),
            pltpu.VMEM((128, 128), F32),
            pltpu.VMEM((128, 128), F32),
            pltpu.VMEM((FIELD, 128), F32),
            dma((4,)), dma((4, 4)), dma((4, 4)), dma((2, 8)), dma((2, 8)),
            dma((8,)), dma((8,)), dma((TA,)), dma((TA,)), dma,
        ],
        compiler_params=pltpu.CompilerParams(
            collective_id=0, has_side_effects=True, vmem_limit_bytes=48 * 1024 * 1024
        ),
    )(
        source.reshape(FIELD, 128),
        gauge_links.reshape(72 * PLANE, 128),
        clover_term.reshape(144 * PLANE, 128),
        null_vectors.reshape(VECS, FIELD, 128),
        owners,
    )
    coarse = coarse.reshape(TA, 8, 128)[:, :2, :4 * VECS].reshape(2 * TA, 4 * VECS).T
    return x.reshape(source.shape), coarse


def solution(mesh):
    in_specs = (
        P(None, "gz", "ta", None),
        P(None, None, "gz", "ta", None),
        P(None, None, None, None, "gz", "ta", None),
        P(None, None, "gz", "ta", None),
        P(("gz", "ta"), None),
    )
    out_specs = (P(None, "gz", "ta", None), P(None, ("gz", "ta")))
    return jax.shard_map(
        on_device, mesh=mesh, in_specs=in_specs, out_specs=out_specs, check_vma=False
    )
```

```python
import jax
import jax.numpy as jnp
from jax import lax
from jax.experimental import pallas as pl
from jax.experimental.pallas import tpu as pltpu
from jax.sharding import PartitionSpec as P

MESH = pl.DeviceIdType.MESH
F32 = jnp.float32
BF16 = jnp.bfloat16

NZ = 4
COMPS = 24
VECS = 24
GZ = 8
TA = 16
PLANE = 32
FIELD = COMPS * PLANE
WEIGHT = 0.24
MASS = 4.2
HALF = 0.5 * WEIGHT
KAPPA = 2.0 / WEIGHT - 2.0 * MASS
X, Y, Z, T = 0, 1, 2, 3

SPIN = {
    X: [[(-1, 1, 1), (-1, 1, 0)], [(1, 0, 1), (1, 0, 0)]],
    Y: [[(1, 0, 1), (-1, 0, 0)], [(1, 1, 1), (-1, 1, 0)]],
    Z: [[(-1, 1, 0), (1, 1, 1)], [(1, 0, 0), (-1, 0, 1)]],
    T: [[(-1, 0, 0), (-1, 0, 1)], [(-1, 1, 0), (-1, 1, 1)]],
}
CORNERS = ((-1, 1), (-1, -1), (1, 1), (1, -1))
INVERSE = {X: -1, Y: -1, Z: -1, T: 1}


NEAR_FIRST = (1, 15, 2, 14, 3, 13, 4, 12, 5, 11, 6, 10, 7, 9, 8)
FAR_FIRST = (8, 7, 9, 6, 10, 5, 11, 4, 12, 3, 13, 2, 14, 1, 15)


def comp(reim, spin, colour):
    return 12 * reim + 3 * spin + colour


def half(reim, spin, colour):
    return 6 * reim + 3 * spin + colour


def add(a, b, sign):
    return a + b if sign > 0 else a - b


def project(load, direction, parity, s):
    out = []
    for r in range(2):
        sign, r2, s2 = SPIN[direction][r][s]
        out.append([add(load(r, s, c), load(r2, 2 + s2, c), -parity * sign) for c in range(3)])
    return out


def colour(link, a, dagger):
    re, im = [], []
    for row in range(3):
        tr = ti = None
        for k in range(3):
            e = 3 * k + row if dagger else 3 * row + k
            lr, li = link[e], link[9 + e]
            if dagger:
                nr = lr * a[0][k] + li * a[1][k]
                ni = lr * a[1][k] - li * a[0][k]
            else:
                nr = lr * a[0][k] - li * a[1][k]
                ni = lr * a[1][k] + li * a[0][k]
            tr = nr if tr is None else tr + nr
            ti = ni if ti is None else ti + ni
        re.append(tr)
        im.append(ti)
    return [re, im]


def lower_terms(direction, s):
    out = []
    for r in range(2):
        for spin in range(2):
            sign, r2, s2 = SPIN[direction][r][spin]
            if s2 == s:
                out.append((INVERSE[direction] * sign, r2, r, 2 + spin))
    return out


def kernel(
    source, links, clover, vectors, owners, x_out, coarse_out,
    y, g, cl, v, sz, st, sr, sl, ll, rz, rt, rd, rl, tmp, wt, inner, place, so, rc, xs,
    load_sem, msg_send, msg_recv, diag_send, diag_recv, link_send, link_recv, all_send, all_recv, x_sem,
):
    me_z = lax.axis_index("gz")
    me_t = lax.axis_index("ta")

    def device(dz, dt):
        return (lax.rem(me_z + (dz + GZ), GZ), lax.rem(me_t + (dt + TA), TA))

    def prepare():
        sub = lax.broadcasted_iota(jnp.int32, (16, 128), 0)
        lane = lax.broadcasted_iota(jnp.int32, (16, 128), 1)
        padded = jnp.concatenate([owners[...].astype(F32), jnp.full((1, 112), -1.0, F32)], axis=1)
        own_row = jnp.broadcast_to(padded, (16, 128))
        own = jnp.sum(jnp.where(sub == lane, own_row, 0.0), axis=1, keepdims=True)
        rank = jnp.sum(jnp.where((own == own_row) & (lane < sub), 1.0, 0.0), axis=1, keepdims=True)
        slot = own * 8.0 + rank
        for part in range(2):
            agg = ((lane & 7) >> 2) * 8 + ((lane >> 4) & 7)
            of_lane = jnp.sum(jnp.where(agg == sub, slot, 0.0), axis=0, keepdims=True)
            row = lax.broadcasted_iota(jnp.int32, (128, 128), 0).astype(F32)
            place[:, 128 * part:128 * (part + 1)] = jnp.where(row == of_lane, 1.0, 0.0)

        for j in range(16):
            for e in (0, 8, 16):
                diag = lax.broadcasted_iota(jnp.int32, (8, 128), 0) + e
                rl[pl.ds(24 * j + e, 8), :] = jnp.where(
                    (diag == 0) | (diag == 4) | (diag == 8), jnp.ones((8, 128), F32), 0.0
                )

    half_links = 36 * PLANE
    loads = [
        pltpu.make_async_copy(source, y.at[pl.ds(0, FIELD)], load_sem.at[0]),
        pltpu.make_async_copy(links.at[pl.ds(half_links, half_links)], g.at[pl.ds(half_links, half_links)], load_sem.at[1]),
        pltpu.make_async_copy(links.at[pl.ds(0, half_links)], g.at[pl.ds(0, half_links)], load_sem.at[2]),
        pltpu.make_async_copy(clover, cl, load_sem.at[3]),
        pltpu.make_async_copy(vectors, v, load_sem.at[4]),
    ]
    for c in loads[:4]:
        c.start()

    barrier = pltpu.get_barrier_semaphore()
    greet = [(dz, dt) for dz in (-1, 1) for dt in (0, -1, 1)] + [(0, dt) for dt in NEAR_FIRST]
    for dz, dt in greet:
        pl.semaphore_signal(barrier, inc=1, device_id=device(dz, dt), device_id_type=MESH)

    down_sign = jnp.where(me_t == 0, -1.0, 1.0).astype(F32)
    up_sign = jnp.where(me_t == TA - 1, -1.0, 1.0).astype(F32)

    def yrow(k, c, z, t=0):
        return k * FIELD + c * PLANE + z * 8 + t

    def y_at(k, z):
        def load(r, s, c):
            return y[pl.ds(pl.multiple_of(yrow(k, comp(r, s, c), z), 8), 8), :]
        return load

    def link_at(direction, z):
        return [
            g[pl.ds(pl.multiple_of((18 * direction + e) * PLANE + z * 8, 8), 8), :]
            for e in range(18)
        ]

    def bump(k, z, r, s, c, value, sign=1):
        at = pl.ds(pl.multiple_of(yrow(k, comp(r, s, c), z), 8), 8)
        y[at, :] = add(y[at, :], value, sign)

    y_lane = lax.broadcasted_iota(jnp.int32, (8, 128), 1) & 15
    t_row = lax.broadcasted_iota(jnp.int32, (8, 128), 0)

    def ahead(direction, a):
        if direction == X:
            return pltpu.roll(a, 112, 1)
        if direction == Y:
            return jnp.where(y_lane == 15, pltpu.roll(a, 15, 1), pltpu.roll(a, 127, 1))
        return jnp.where(t_row == 7, 0.0, pltpu.roll(a, 7, 0))

    def behind(direction, a):
        if direction == X:
            return pltpu.roll(a, 16, 1)
        if direction == Y:
            return jnp.where(y_lane == 0, pltpu.roll(a, 113, 1), pltpu.roll(a, 1, 1))
        return jnp.where(t_row == 0, 0.0, pltpu.roll(a, 1, 0))

    def layer(k, z):
        load = y_at(k, z)
        for h in range(2):
            vr = [load(0, 2 * h + i // 3, i % 3) for i in range(6)]
            vi = [load(1, 2 * h + i // 3, i % 3) for i in range(6)]
            ur = [-2.0 * a for a in vr]
            ui = [-2.0 * a for a in vi]
            for row in range(6):
                tr = KAPPA * vr[row]
                ti = KAPPA * vi[row]
                for k2 in range(6):
                    base = ((2 * h) * 6 + row) * 6 + k2
                    cr = cl[pl.ds(pl.multiple_of(base * PLANE + z * 8, 8), 8), :]
                    ci = cl[pl.ds(pl.multiple_of((base + 36) * PLANE + z * 8, 8), 8), :]
                    tr = tr + (cr * ur[k2] - ci * ui[k2])
                    ti = ti + (cr * ui[k2] + ci * ur[k2])
                s, c = 2 * h + row // 3, row % 3
                y[pl.ds(pl.multiple_of(yrow(k + 1, comp(0, s, c), z), 8), 8), :] = tr
                y[pl.ds(pl.multiple_of(yrow(k + 1, comp(1, s, c), z), 8), 8), :] = ti
        for direction in (X, Y, T):
            link = link_at(direction, z)
            for s in range(2):
                fwd = project(load, direction, -1, s)
                fwd = [[ahead(direction, a) for a in part] for part in fwd]
                fwd = colour(link, fwd, False)
                bwd = colour(link, project(load, direction, 1, s), True)
                bwd = [[behind(direction, a) for a in part] for part in bwd]
                for r in range(2):
                    for c in range(3):
                        bump(k + 1, z, r, s, c, fwd[r][c] + bwd[r][c])
                for sign, r2, r, s2 in lower_terms(direction, s):
                    for c in range(3):
                        bump(k + 1, z, r, s2, c, fwd[r2][c] - bwd[r2][c], sign)

    def z_forward(k, z):
        link = link_at(Z, z)
        for s in range(2):
            put_half(k + 1, z, s, colour(link, project(y_at(k, z + 1), Z, -1, s), False), 1)

    def z_backward(k, z):
        link = link_at(Z, z)
        for s in range(2):
            put_half(k + 1, z + 1, s, colour(link, project(y_at(k, z), Z, 1, s), True), -1)

    def put_half(k, z, s, w, parity):
        for r in range(2):
            for c in range(3):
                bump(k, z, r, s, c, w[r][c])
        for sign, r2, r, s2 in lower_terms(Z, s):
            for c in range(3):
                bump(k, z, r, s2, c, w[r2][c], parity * sign)

    def local(k, first, at_third):
        def step(i, carry):
            @pl.when(i == 2)
            def _():
                at_third()
            layer(k, lax.rem(i + first, NZ))
            return carry
        lax.fori_loop(0, NZ, step, 0)

    def rows_of(k, t):
        def load(r, s, c):
            return y[pl.ds(yrow(k, comp(r, s, c), 0, t), NZ, stride=8), :]
        return load

    def link_rows(t):
        return [g[pl.ds((18 * T + e) * PLANE + t, NZ, stride=8), :] for e in range(18)]

    def pack_z(k):
        link = link_at(Z, NZ - 1)
        for s in range(2):
            dn = project(y_at(k, 0), Z, -1, s)
            up = colour(link, project(y_at(k, NZ - 1), Z, 1, s), True)
            for r in range(2):
                for c in range(3):
                    sz[k, 0, pl.ds(8 * half(r, s, c), 8), :] = dn[r][c]
                    sz[k, 1, pl.ds(8 * half(r, s, c), 8), :] = up[r][c]
        message(k, 0).start()
        message(k, 1).start()

    def pack_t(k):
        tlink = link_rows(7)
        for s in range(2):
            dn = project(rows_of(k, 0), T, -1, s)
            up = colour(tlink, project(rows_of(k, 7), T, 1, s), True)
            for r in range(2):
                for c in range(3):
                    at = pl.ds(half(r, s, c), NZ, stride=12)
                    st[k, 0, at, :] = dn[r][c] * down_sign
                    st[k, 1, at, :] = up[r][c] * up_sign
        message(k, 2).start()
        message(k, 3).start()

    def pack_corners(p, k):
        for i, (dz, dt) in enumerate(CORNERS):
            m = 1 if dt > 0 else 0
            z = NZ - 1 if dz > 0 else 0
            sr[p, i, pl.ds(0, 12), :] = st[k, m, pl.ds(12 * z, 12), :]
            t, sign = (7, up_sign) if dt > 0 else (0, down_sign)
            sr[p, i, pl.ds(12, 12), :] = sz[k, 1 if dz > 0 else 0, pl.ds(t, 12, stride=8), :] * sign
            corner(p, i).start()

    def message(k, m):
        target = ((-1, 0), (1, 0), (0, -1), (0, 1))[m]
        src, dst = (sz, rz) if m < 2 else (st, rt)
        return pltpu.make_async_remote_copy(
            src_ref=src.at[k, m % 2], dst_ref=dst.at[k, m % 2],
            send_sem=msg_send.at[k, m], recv_sem=msg_recv.at[k, m],
            device_id=device(*target), device_id_type=MESH,
        )

    def corner(p, i):
        return pltpu.make_async_remote_copy(
            src_ref=sr.at[p, i], dst_ref=rd.at[p, pl.ds(24 * i, 24)],
            send_sem=diag_send.at[p, i], recv_sem=diag_recv.at[p, i],
            device_id=device(*CORNERS[i]), device_id_type=MESH,
        )

    def corner_link(i):
        block, count, target, to = ((0, 1, (-1, 0), 0), (1, 3, (1, 0), 1), (2, 1, (0, -1), 4), (3, 3, (0, 1), 5))[i]
        return pltpu.make_async_remote_copy(
            src_ref=sl.at[pl.ds(block, count)], dst_ref=ll.at[pl.ds(to, count)],
            send_sem=link_send.at[i], recv_sem=link_recv.at[i],
            device_id=device(*target), device_id_type=MESH,
        )

    def finish_t(k):
        link = link_rows(7)
        for s in range(2):
            a = [[rt[k, 0, pl.ds(half(r, s, c), NZ, stride=12), :] for c in range(3)] for r in range(2)]
            b = [[rt[k, 1, pl.ds(half(r, s, c), NZ, stride=12), :] for c in range(3)] for r in range(2)]
            for w, t, parity in ((colour(link, a, False), 7, 1), (b, 0, -1)):
                def bump_row(r, s, c, value, sign):
                    at = pl.ds(yrow(k + 1, comp(r, s, c), 0, t), NZ, stride=8)
                    y[at, :] = add(y[at, :], value, sign)
                for r in range(2):
                    for c in range(3):
                        bump_row(r, s, c, w[r][c], 1)
                for sign, r2, r, s2 in lower_terms(T, s):
                    for c in range(3):
                        bump_row(r, s2, c, w[r2][c], parity * sign)

    def finish_z(k):
        link = link_at(Z, NZ - 1)
        for s in range(2):
            a = [[rz[k, 0, pl.ds(8 * half(r, s, c), 8), :] for c in range(3)] for r in range(2)]
            put_half(k + 1, NZ - 1, s, colour(link, a, False), 1)
            b = [[rz[k, 1, pl.ds(8 * half(r, s, c), 8), :] for c in range(3)] for r in range(2)]
            put_half(k + 1, 0, s, b, -1)

    def correct(p):
        one = [rl[pl.ds(e, 8, stride=24), :] for e in range(18)]
        two = [rl[pl.ds(192 + e, 8, stride=24), :] for e in range(18)]
        j = lax.broadcasted_iota(jnp.int32, (8, 128), 0)
        plus = (j == 0) | (j == 3) | (j == 5) | (j == 6)
        sign_j = jnp.where(plus, jnp.ones((8, 128), F32), -1.0)
        w = []
        for s in range(2):
            a = [[rd[p, pl.ds(half(r, s, c), 8, stride=12), :] for c in range(3)] for r in range(2)]
            w.append(colour(one, a, False))
        for s in range(2):
            q = []
            for r in range(2):
                sign, r2, s2 = SPIN[Z][r][s]
                q.append([add(w[s][r][c], sign_j * w[s2][r2][c], sign) for c in range(3)])
            q = colour(two, q, True)
            for r in range(2):
                for c in range(3):
                    tmp[pl.ds(8 * half(r, s, c), 8), :] = q[r][c]

    def correct_z(k):
        for n in range(12):
            for m in range(2):
                at = pl.ds(8 * n, 2, stride=7)
                rz[k, m, at, :] = rz[k, m, at, :] + tmp[pl.ds(8 * n + 4 * m, 2, stride=2), :]

    def correct_t(k):
        for n in range(12):
            for m, z, pos in ((0, 0, 7), (0, 3, 3), (1, 0, 5), (1, 3, 1)):
                at = pl.ds(12 * z + n, 1)
                rt[k, m, at, :] = rt[k, m, at, :] + tmp[pl.ds(8 * n + pos, 1), :]

    def regroup(n, carry):
        for c in range(COMPS):
            f = v[n, pl.ds(c * PLANE, PLANE), :].astype(F32)
            v[n, pl.ds(c * PLANE, PLANE), :] = jnp.concatenate([f[8:24], f[:8], f[24:]], axis=0).astype(BF16)
        return carry

    def products(part, h):
        site = lax.broadcasted_iota(jnp.int32, (16, 128), 1)
        group = (site >> 6) * 4 + ((site & 15) >> 2)
        scale = HALF ** 4
        left = []
        for c in range(6):
            rows = []
            for r in range(2):
                n = comp(r, 2 * h, 0) + c
                if part == 0:
                    field = y[pl.ds(yrow(4, n, 1), 16), :]
                else:
                    field = jnp.concatenate([y[pl.ds(yrow(4, n, 0), 8), :], y[pl.ds(yrow(4, n, 3), 8), :]], axis=0)
                rows.append((field * scale).astype(BF16))
                left.append(v[:, pl.ds(n * PLANE + 16 * part, 16), :].reshape(VECS * 16, 128))
            for grp in range(8):
                keep = (group == grp).astype(F32).astype(BF16)
                re, im = rows[0] * keep, rows[1] * keep
                col = 256 * c
                wt[2 * part + h, pl.ds(16 * grp, 16), col:col + 128] = re
                wt[2 * part + h, pl.ds(16 * grp, 16), col + 128:col + 256] = im
                wt[2 * part + h, pl.ds(128 + 16 * grp, 16), col:col + 128] = im
                wt[2 * part + h, pl.ds(128 + 16 * grp, 16), col + 128:col + 256] = -re
        return lax.dot_general(
            jnp.concatenate(left, axis=1), wt[2 * part + h], (((1,), (1,)), ((), ())), preferred_element_type=F32
        )

    loads[0].wait()
    loads[1].wait()
    corner_rows = ((T, 0, 7), (T, 3, 7), (Z, 3, 0), (Z, 3, 7))
    for i in range(6):
        direction, z, t = corner_rows[i % 4]
        for e, count in ((0, 8), (8, 8), (16, 2)):
            sl[i, pl.ds(e, count), :] = g[pl.ds((18 * direction + e) * PLANE + z * 8 + t, count, stride=32), :]
    pl.semaphore_wait(barrier, len(greet))

    for p in range(2):
        k = 2 * p
        pack_z(k)
        pack_t(k)
        pack_corners(p, k)
        if p == 0:
            for i in range(4):
                corner_link(i).start()
            loads[2].wait()
            loads[3].wait()
            loads[4].start()
            prepare()

        def faces():
            z_backward(k, NZ - 2)
            z_forward(k, 0)
            pack_z(k + 1)
        local(k, NZ - 1, faces)
        z_forward(k, 1)
        z_forward(k, 2)
        z_backward(k, 0)
        z_backward(k, 1)
        pack_t(k + 1)
        if p == 0:
            loads[4].wait()
            lax.fori_loop(0, VECS, regroup, 0)
        message(k, 2).wait_recv()
        message(k, 3).wait_recv()
        finish_t(k)

        def halo():
            z_forward(k + 1, 1)
            z_backward(k + 1, 1)
            message(k, 0).wait_recv()
            message(k, 1).wait_recv()
            finish_z(k)
        local(k + 1, 1, halo)
        z_forward(k + 1, 0)
        z_forward(k + 1, 2)
        z_backward(k + 1, 0)
        z_backward(k + 1, 2)
        for i in range(4):
            corner(p, i).wait_recv()
        if p == 0:
            for i in range(4):
                corner_link(i).wait_recv()
            for i, to in enumerate((2, 6, 8 + 4, 8 + 6, 3, 1, 8 + 5, 8 + 1)):
                rl[pl.ds(24 * to, 24), :] = ll[i]
        correct(p)
        message(k + 1, 2).wait_recv()
        message(k + 1, 3).wait_recv()
        correct_t(k + 1)
        finish_t(k + 1)
        if p == 1:
            for h in range(2):
                inner[h] = products(0, h)
        message(k + 1, 0).wait_recv()
        message(k + 1, 1).wait_recv()
        correct_z(k + 1)
        finish_z(k + 1)

    pooled = []
    i0 = lax.broadcasted_iota(jnp.int32, (VECS * 16, 256), 0) & 15
    i1 = lax.broadcasted_iota(jnp.int32, (VECS * 16, 256), 1) & 15
    for h in range(2):
        prod = jnp.where(i0 == i1, inner[h] + products(1, h), 0.0)
        pooled.append(jnp.sum(prod.reshape(VECS, 16, 256), axis=1))
    zero = jnp.zeros((2 * VECS, 128), F32)
    pooled = jnp.concatenate(pooled, axis=0)
    first = jnp.concatenate([pooled[:, :128], zero], axis=1)
    second = jnp.concatenate([zero, pooled[:, 128:]], axis=1)
    values = jnp.concatenate([first, second, jnp.zeros((32, 256), F32)], axis=0)
    so[...] = lax.dot_general(
        place[...], values, (((1,), (1,)), ((), ())), preferred_element_type=F32,
        precision=lax.Precision.HIGHEST,
    )

    def exchange(d):
        to = lax.rem(me_t + d, TA)
        return pltpu.make_async_remote_copy(
            src_ref=so.at[pl.ds(pl.multiple_of(8 * to, 8), 8)],
            dst_ref=rc.at[pl.ds(pl.multiple_of(8 * me_t, 8), 8)],
            send_sem=all_send.at[d], recv_sem=all_recv.at[d],
            device_id=(me_z, to), device_id_type=MESH,
        )

    for d in FAR_FIRST:
        exchange(d).start()
    mine = pl.ds(pl.multiple_of(8 * me_t, 8), 8)
    rc[mine, :] = so[mine, :]

    def solution_rows(i, carry):
        at = [pl.ds(pl.multiple_of(n * FIELD + i * 32, 8), 32) for n in range(4)]
        total = y[at[2], :] + HALF * y[at[3], :]
        total = y[at[1], :] + HALF * total
        total = y[at[0], :] + HALF * total
        xs[at[0], :] = WEIGHT * total
        return carry
    lax.fori_loop(0, COMPS, solution_rows, 0)
    write = pltpu.make_async_copy(xs, x_out, x_sem)
    write.start()

    for d in range(1, TA):
        exchange(d).wait()
    coarse_out[...] = rc[...]
    for p in range(2):
        for m in range(4):
            message(2 * p, m).wait_send()
            message(2 * p + 1, m).wait_send()
        for i in range(4):
            corner(p, i).wait_send()
    for i in range(4):
        corner_link(i).wait_send()
    write.wait()


def on_device(source, gauge_links, clover_term, null_vectors, owners):
    hbm = pl.BlockSpec(memory_space=pltpu.HBM)
    vmem = pl.BlockSpec(memory_space=pltpu.VMEM)
    dma = pltpu.SemaphoreType.DMA
    x, coarse = pl.pallas_call(
        kernel,
        out_shape=(jax.ShapeDtypeStruct((FIELD, 128), F32), jax.ShapeDtypeStruct((128, 128), F32)),
        in_specs=[hbm, hbm, hbm, hbm, vmem],
        out_specs=(pl.BlockSpec(memory_space=pl.ANY), vmem),
        scratch_shapes=[
            pltpu.VMEM((5 * FIELD, 128), F32),
            pltpu.VMEM((72 * PLANE, 128), F32),
            pltpu.VMEM((144 * PLANE, 128), F32),
            pltpu.VMEM((VECS, FIELD, 128), BF16),
            pltpu.VMEM((4, 2, 96, 128), F32),
            pltpu.VMEM((4, 2, 48, 128), F32),
            pltpu.VMEM((2, 4, 24, 128), F32),
            pltpu.VMEM((6, 24, 128), F32),
            pltpu.VMEM((8, 24, 128), F32),
            pltpu.VMEM((4, 2, 96, 128), F32),
            pltpu.VMEM((4, 2, 48, 128), F32),
            pltpu.VMEM((2, 96, 128), F32),
            pltpu.VMEM((16 * 24, 128), F32),
            pltpu.VMEM((96, 128), F32),
            pltpu.VMEM((4, 256, 1536), BF16),
            pltpu.VMEM((2, VECS * 16, 256), F32),
            pltpu.VMEM((128, 256), F32),
            pltpu.VMEM((128, 128), F32),
            pltpu.VMEM((128, 128), F32),
            pltpu.VMEM((FIELD, 128), F32),
            dma((5,)), dma((4, 4)), dma((4, 4)), dma((2, 4)), dma((2, 4)),
            dma((4,)), dma((4,)), dma((TA,)), dma((TA,)), dma,
        ],
        compiler_params=pltpu.CompilerParams(
            collective_id=0, has_side_effects=True, vmem_limit_bytes=63 * 1024 * 1024
        ),
    )(
        source.reshape(FIELD, 128),
        gauge_links.reshape(72 * PLANE, 128),
        clover_term.reshape(144 * PLANE, 128),
        null_vectors.reshape(VECS, FIELD, 128),
        owners.reshape(1, 16),
    )
    coarse = coarse.reshape(TA, 8, 128)[:, :2, :4 * VECS].reshape(2 * TA, 4 * VECS).T
    return x.reshape(source.shape), coarse


def solution(mesh):
    in_specs = (
        P(None, "gz", "ta", None),
        P(None, None, "gz", "ta", None),
        P(None, None, None, None, "gz", "ta", None),
        P(None, None, "gz", "ta", None),
        P(("gz", "ta"), None),
    )
    out_specs = (P(None, "gz", "ta", None), P(None, ("gz", "ta")))
    return jax.shard_map(
        on_device, mesh=mesh, in_specs=in_specs, out_specs=out_specs, check_vma=False
    )
```

```python
import jax
import jax.numpy as jnp
from jax import lax
from jax.experimental import pallas as pl
from jax.experimental.pallas import tpu as pltpu
from jax.sharding import PartitionSpec as P

MESH = pl.DeviceIdType.MESH
F32 = jnp.float32
BF16 = jnp.bfloat16

NZ = 4
COMPS = 24
VECS = 24
GZ = 8
TA = 16
PLANE = 32
FIELD = COMPS * PLANE
WEIGHT = 0.24
MASS = 4.2
HALF = 0.5 * WEIGHT
KAPPA = 2.0 / WEIGHT - 2.0 * MASS
X, Y, Z, T = 0, 1, 2, 3

SPIN = {
    X: [[(-1, 1, 1), (-1, 1, 0)], [(1, 0, 1), (1, 0, 0)]],
    Y: [[(1, 0, 1), (-1, 0, 0)], [(1, 1, 1), (-1, 1, 0)]],
    Z: [[(-1, 1, 0), (1, 1, 1)], [(1, 0, 0), (-1, 0, 1)]],
    T: [[(-1, 0, 0), (-1, 0, 1)], [(-1, 1, 0), (-1, 1, 1)]],
}
CORNERS = ((-1, 1), (-1, -1), (1, 1), (1, -1))
INVERSE = {X: -1, Y: -1, Z: -1, T: 1}


NEAR_FIRST = (1, 15, 2, 14, 3, 13, 4, 12, 5, 11, 6, 10, 7, 9, 8)
FAR_FIRST = (8, 7, 9, 6, 10, 5, 11, 4, 12, 3, 13, 2, 14, 1, 15)


def comp(reim, spin, colour):
    return 12 * reim + 3 * spin + colour


def half(reim, spin, colour):
    return 6 * reim + 3 * spin + colour


def add(a, b, sign):
    return a + b if sign > 0 else a - b


def project(load, direction, parity, s):
    out = []
    for r in range(2):
        sign, r2, s2 = SPIN[direction][r][s]
        out.append([add(load(r, s, c), load(r2, 2 + s2, c), -parity * sign) for c in range(3)])
    return out


def colour(link, a, dagger):
    re, im = [], []
    for row in range(3):
        tr = ti = None
        for k in range(3):
            e = 3 * k + row if dagger else 3 * row + k
            lr, li = link[e], link[9 + e]
            if dagger:
                nr = lr * a[0][k] + li * a[1][k]
                ni = lr * a[1][k] - li * a[0][k]
            else:
                nr = lr * a[0][k] - li * a[1][k]
                ni = lr * a[1][k] + li * a[0][k]
            tr = nr if tr is None else tr + nr
            ti = ni if ti is None else ti + ni
        re.append(tr)
        im.append(ti)
    return [re, im]


def lower_terms(direction, s):
    out = []
    for r in range(2):
        for spin in range(2):
            sign, r2, s2 = SPIN[direction][r][spin]
            if s2 == s:
                out.append((INVERSE[direction] * sign, r2, r, 2 + spin))
    return out


def kernel(
    source, links, clover, vectors, owners, x_out, coarse_out,
    y, g, cl, v, sz, st, sr, sl, ll, rz, rt, rd, rl, tmp, wt, inner, place, so, rc, ow,
    load_sem, msg_send, msg_recv, diag_send, diag_recv, link_send, link_recv, all_send, all_recv,
):
    me_z = lax.axis_index("gz")
    me_t = lax.axis_index("ta")

    def device(dz, dt):
        return (lax.rem(me_z + (dz + GZ), GZ), lax.rem(me_t + (dt + TA), TA))

    def prepare():
        loads[5].wait()
        sub = lax.broadcasted_iota(jnp.int32, (16, 128), 0)
        lane = lax.broadcasted_iota(jnp.int32, (16, 128), 1)
        padded = jnp.concatenate([ow[...].astype(F32), jnp.full((1, 112), -1.0, F32)], axis=1)
        own_row = jnp.broadcast_to(padded, (16, 128))
        own = jnp.sum(jnp.where(sub == lane, own_row, 0.0), axis=1, keepdims=True)
        rank = jnp.sum(jnp.where((own == own_row) & (lane < sub), 1.0, 0.0), axis=1, keepdims=True)
        slot = own * 8.0 + rank
        for part in range(2):
            agg = ((lane & 7) >> 2) * 8 + ((lane >> 4) & 7)
            of_lane = jnp.sum(jnp.where(agg == sub, slot, 0.0), axis=0, keepdims=True)
            row = lax.broadcasted_iota(jnp.int32, (128, 128), 0).astype(F32)
            place[:, 128 * part:128 * (part + 1)] = jnp.where(row == of_lane, 1.0, 0.0)

        for j in range(16):
            for e in (0, 8, 16):
                diag = lax.broadcasted_iota(jnp.int32, (8, 128), 0) + e
                rl[pl.ds(24 * j + e, 8), :] = jnp.where(
                    (diag == 0) | (diag == 4) | (diag == 8), jnp.ones((8, 128), F32), 0.0
                )

    half_links = 36 * PLANE
    loads = [
        pltpu.make_async_copy(source, y.at[pl.ds(0, FIELD)], load_sem.at[0]),
        pltpu.make_async_copy(links.at[pl.ds(half_links, half_links)], g.at[pl.ds(half_links, half_links)], load_sem.at[1]),
        pltpu.make_async_copy(links.at[pl.ds(0, half_links)], g.at[pl.ds(0, half_links)], load_sem.at[2]),
        pltpu.make_async_copy(clover, cl, load_sem.at[3]),
        pltpu.make_async_copy(vectors, v, load_sem.at[4]),
        pltpu.make_async_copy(owners, ow, load_sem.at[5]),
    ]
    for c in loads[:4]:
        c.start()

    barrier = pltpu.get_barrier_semaphore()
    greet = [(dz, dt) for dz in (-1, 1) for dt in (0, -1, 1)] + [(0, dt) for dt in NEAR_FIRST]
    for dz, dt in greet:
        pl.semaphore_signal(barrier, inc=1, device_id=device(dz, dt), device_id_type=MESH)

    down_sign = jnp.where(me_t == 0, -1.0, 1.0).astype(F32)
    up_sign = jnp.where(me_t == TA - 1, -1.0, 1.0).astype(F32)

    def yrow(k, c, z, t=0):
        return k * FIELD + c * PLANE + z * 8 + t

    def y_at(k, z):
        def load(r, s, c):
            return y[pl.ds(pl.multiple_of(yrow(k, comp(r, s, c), z), 8), 8), :]
        return load

    def link_at(direction, z):
        return [
            g[pl.ds(pl.multiple_of((18 * direction + e) * PLANE + z * 8, 8), 8), :]
            for e in range(18)
        ]

    def bump(k, z, r, s, c, value, sign=1):
        at = pl.ds(pl.multiple_of(yrow(k, comp(r, s, c), z), 8), 8)
        y[at, :] = add(y[at, :], value, sign)

    y_lane = lax.broadcasted_iota(jnp.int32, (8, 128), 1) & 15
    t_row = lax.broadcasted_iota(jnp.int32, (8, 128), 0)

    def ahead(direction, a):
        if direction == X:
            return pltpu.roll(a, 112, 1)
        if direction == Y:
            return jnp.where(y_lane == 15, pltpu.roll(a, 15, 1), pltpu.roll(a, 127, 1))
        return jnp.where(t_row == 7, 0.0, pltpu.roll(a, 7, 0))

    def behind(direction, a):
        if direction == X:
            return pltpu.roll(a, 16, 1)
        if direction == Y:
            return jnp.where(y_lane == 0, pltpu.roll(a, 113, 1), pltpu.roll(a, 1, 1))
        return jnp.where(t_row == 0, 0.0, pltpu.roll(a, 1, 0))

    def layer(k, z):
        load = y_at(k, z)
        for h in range(2):
            vr = [load(0, 2 * h + i // 3, i % 3) for i in range(6)]
            vi = [load(1, 2 * h + i // 3, i % 3) for i in range(6)]
            ur = [-2.0 * a for a in vr]
            ui = [-2.0 * a for a in vi]
            for row in range(6):
                tr = KAPPA * vr[row]
                ti = KAPPA * vi[row]
                for k2 in range(6):
                    base = ((2 * h) * 6 + row) * 6 + k2
                    cr = cl[pl.ds(pl.multiple_of(base * PLANE + z * 8, 8), 8), :]
                    ci = cl[pl.ds(pl.multiple_of((base + 36) * PLANE + z * 8, 8), 8), :]
                    tr = tr + (cr * ur[k2] - ci * ui[k2])
                    ti = ti + (cr * ui[k2] + ci * ur[k2])
                s, c = 2 * h + row // 3, row % 3
                y[pl.ds(pl.multiple_of(yrow(k + 1, comp(0, s, c), z), 8), 8), :] = tr
                y[pl.ds(pl.multiple_of(yrow(k + 1, comp(1, s, c), z), 8), 8), :] = ti
        for direction in (X, Y, T):
            link = link_at(direction, z)
            for s in range(2):
                fwd = project(load, direction, -1, s)
                fwd = [[ahead(direction, a) for a in part] for part in fwd]
                fwd = colour(link, fwd, False)
                bwd = colour(link, project(load, direction, 1, s), True)
                bwd = [[behind(direction, a) for a in part] for part in bwd]
                for r in range(2):
                    for c in range(3):
                        bump(k + 1, z, r, s, c, fwd[r][c] + bwd[r][c])
                for sign, r2, r, s2 in lower_terms(direction, s):
                    for c in range(3):
                        bump(k + 1, z, r, s2, c, fwd[r2][c] - bwd[r2][c], sign)

    def z_forward(k, z):
        link = link_at(Z, z)
        for s in range(2):
            put_half(k + 1, z, s, colour(link, project(y_at(k, z + 1), Z, -1, s), False), 1)

    def z_backward(k, z):
        link = link_at(Z, z)
        for s in range(2):
            put_half(k + 1, z + 1, s, colour(link, project(y_at(k, z), Z, 1, s), True), -1)

    def put_half(k, z, s, w, parity):
        for r in range(2):
            for c in range(3):
                bump(k, z, r, s, c, w[r][c])
        for sign, r2, r, s2 in lower_terms(Z, s):
            for c in range(3):
                bump(k, z, r, s2, c, w[r2][c], parity * sign)

    def local(k, first, at_third):
        def step(i, carry):
            @pl.when(i == 2)
            def _():
                at_third()
            layer(k, lax.rem(i + first, NZ))
            return carry
        lax.fori_loop(0, NZ, step, 0)

    def rows_of(k, t):
        def load(r, s, c):
            return y[pl.ds(yrow(k, comp(r, s, c), 0, t), NZ, stride=8), :]
        return load

    def link_rows(t):
        return [g[pl.ds((18 * T + e) * PLANE + t, NZ, stride=8), :] for e in range(18)]

    def pack_z(k):
        link = link_at(Z, NZ - 1)
        for s in range(2):
            dn = project(y_at(k, 0), Z, -1, s)
            up = colour(link, project(y_at(k, NZ - 1), Z, 1, s), True)
            for r in range(2):
                for c in range(3):
                    sz[k, 0, pl.ds(8 * half(r, s, c), 8), :] = dn[r][c]
                    sz[k, 1, pl.ds(8 * half(r, s, c), 8), :] = up[r][c]
        message(k, 0).start()
        message(k, 1).start()

    def pack_t(k):
        tlink = link_rows(7)
        for s in range(2):
            dn = project(rows_of(k, 0), T, -1, s)
            up = colour(tlink, project(rows_of(k, 7), T, 1, s), True)
            for r in range(2):
                for c in range(3):
                    at = pl.ds(half(r, s, c), NZ, stride=12)
                    st[k, 0, at, :] = dn[r][c] * down_sign
                    st[k, 1, at, :] = up[r][c] * up_sign
        message(k, 2).start()
        message(k, 3).start()

    def pack_corners(p, k):
        for i, (dz, dt) in enumerate(CORNERS):
            m = 1 if dt > 0 else 0
            z = NZ - 1 if dz > 0 else 0
            sr[p, i, pl.ds(0, 12), :] = st[k, m, pl.ds(12 * z, 12), :]
            t, sign = (7, up_sign) if dt > 0 else (0, down_sign)
            sr[p, i, pl.ds(12, 12), :] = sz[k, 1 if dz > 0 else 0, pl.ds(t, 12, stride=8), :] * sign
            corner(p, i).start()

    def message(k, m):
        target = ((-1, 0), (1, 0), (0, -1), (0, 1))[m]
        src, dst = (sz, rz) if m < 2 else (st, rt)
        return pltpu.make_async_remote_copy(
            src_ref=src.at[k, m % 2], dst_ref=dst.at[k, m % 2],
            send_sem=msg_send.at[k, m], recv_sem=msg_recv.at[k, m],
            device_id=device(*target), device_id_type=MESH,
        )

    def corner(p, i):
        return pltpu.make_async_remote_copy(
            src_ref=sr.at[p, i], dst_ref=rd.at[p, pl.ds(24 * i, 24)],
            send_sem=diag_send.at[p, i], recv_sem=diag_recv.at[p, i],
            device_id=device(*CORNERS[i]), device_id_type=MESH,
        )

    def corner_link(i):
        block, count, target, to = ((0, 1, (-1, 0), 0), (1, 3, (1, 0), 1), (2, 1, (0, -1), 4), (3, 3, (0, 1), 5))[i]
        return pltpu.make_async_remote_copy(
            src_ref=sl.at[pl.ds(block, count)], dst_ref=ll.at[pl.ds(to, count)],
            send_sem=link_send.at[i], recv_sem=link_recv.at[i],
            device_id=device(*target), device_id_type=MESH,
        )

    def finish_t(k):
        link = link_rows(7)
        for s in range(2):
            a = [[rt[k, 0, pl.ds(half(r, s, c), NZ, stride=12), :] for c in range(3)] for r in range(2)]
            b = [[rt[k, 1, pl.ds(half(r, s, c), NZ, stride=12), :] for c in range(3)] for r in range(2)]
            for w, t, parity in ((colour(link, a, False), 7, 1), (b, 0, -1)):
                def bump_row(r, s, c, value, sign):
                    at = pl.ds(yrow(k + 1, comp(r, s, c), 0, t), NZ, stride=8)
                    y[at, :] = add(y[at, :], value, sign)
                for r in range(2):
                    for c in range(3):
                        bump_row(r, s, c, w[r][c], 1)
                for sign, r2, r, s2 in lower_terms(T, s):
                    for c in range(3):
                        bump_row(r, s2, c, w[r2][c], parity * sign)

    def finish_z(k):
        link = link_at(Z, NZ - 1)
        for s in range(2):
            a = [[rz[k, 0, pl.ds(8 * half(r, s, c), 8), :] for c in range(3)] for r in range(2)]
            put_half(k + 1, NZ - 1, s, colour(link, a, False), 1)
            b = [[rz[k, 1, pl.ds(8 * half(r, s, c), 8), :] for c in range(3)] for r in range(2)]
            put_half(k + 1, 0, s, b, -1)

    def correct(p):
        one = [rl[pl.ds(e, 8, stride=24), :] for e in range(18)]
        two = [rl[pl.ds(192 + e, 8, stride=24), :] for e in range(18)]
        j = lax.broadcasted_iota(jnp.int32, (8, 128), 0)
        plus = (j == 0) | (j == 3) | (j == 5) | (j == 6)
        sign_j = jnp.where(plus, jnp.ones((8, 128), F32), -1.0)
        w = []
        for s in range(2):
            a = [[rd[p, pl.ds(half(r, s, c), 8, stride=12), :] for c in range(3)] for r in range(2)]
            w.append(colour(one, a, False))
        for s in range(2):
            q = []
            for r in range(2):
                sign, r2, s2 = SPIN[Z][r][s]
                q.append([add(w[s][r][c], sign_j * w[s2][r2][c], sign) for c in range(3)])
            q = colour(two, q, True)
            for r in range(2):
                for c in range(3):
                    tmp[pl.ds(8 * half(r, s, c), 8), :] = q[r][c]

    def correct_z(k):
        for n in range(12):
            for m in range(2):
                at = pl.ds(8 * n, 2, stride=7)
                rz[k, m, at, :] = rz[k, m, at, :] + tmp[pl.ds(8 * n + 4 * m, 2, stride=2), :]

    def correct_t(k):
        for n in range(12):
            for m, z, pos in ((0, 0, 7), (0, 3, 3), (1, 0, 5), (1, 3, 1)):
                at = pl.ds(12 * z + n, 1)
                rt[k, m, at, :] = rt[k, m, at, :] + tmp[pl.ds(8 * n + pos, 1), :]

    def regroup(n, carry):
        for c in range(COMPS):
            f = v[n, pl.ds(c * PLANE, PLANE), :].astype(F32)
            v[n, pl.ds(c * PLANE, PLANE), :] = jnp.concatenate([f[8:24], f[:8], f[24:]], axis=0).astype(BF16)
        return carry

    def products(part, h):
        site = lax.broadcasted_iota(jnp.int32, (16, 128), 1)
        group = (site >> 6) * 4 + ((site & 15) >> 2)
        scale = HALF ** 4
        left = []
        for c in range(6):
            rows = []
            for r in range(2):
                n = comp(r, 2 * h, 0) + c
                if part == 0:
                    field = y[pl.ds(yrow(4, n, 1), 16), :]
                else:
                    field = jnp.concatenate([y[pl.ds(yrow(4, n, 0), 8), :], y[pl.ds(yrow(4, n, 3), 8), :]], axis=0)
                rows.append((field * scale).astype(BF16))
                left.append(v[:, pl.ds(n * PLANE + 16 * part, 16), :].reshape(VECS * 16, 128))
            for grp in range(8):
                keep = (group == grp).astype(F32).astype(BF16)
                re, im = rows[0] * keep, rows[1] * keep
                col = 256 * c
                wt[2 * part + h, pl.ds(16 * grp, 16), col:col + 128] = re
                wt[2 * part + h, pl.ds(16 * grp, 16), col + 128:col + 256] = im
                wt[2 * part + h, pl.ds(128 + 16 * grp, 16), col:col + 128] = im
                wt[2 * part + h, pl.ds(128 + 16 * grp, 16), col + 128:col + 256] = -re
        return lax.dot_general(
            jnp.concatenate(left, axis=1), wt[2 * part + h], (((1,), (1,)), ((), ())), preferred_element_type=F32
        )

    loads[0].wait()
    loads[1].wait()
    corner_rows = ((T, 0, 7), (T, 3, 7), (Z, 3, 0), (Z, 3, 7))
    for i in range(6):
        direction, z, t = corner_rows[i % 4]
        for e, count in ((0, 8), (8, 8), (16, 2)):
            sl[i, pl.ds(e, count), :] = g[pl.ds((18 * direction + e) * PLANE + z * 8 + t, count, stride=32), :]
    pl.semaphore_wait(barrier, len(greet))

    for p in range(2):
        k = 2 * p
        pack_z(k)
        pack_t(k)
        pack_corners(p, k)
        if p == 0:
            for i in range(4):
                corner_link(i).start()
            loads[2].wait()
            loads[3].wait()
            loads[4].start()
            loads[5].start()
            prepare()

        def faces():
            z_backward(k, NZ - 2)
            z_forward(k, 0)
            pack_z(k + 1)
        local(k, NZ - 1, faces)
        z_forward(k, 1)
        z_forward(k, 2)
        z_backward(k, 0)
        z_backward(k, 1)
        pack_t(k + 1)
        if p == 0:
            loads[4].wait()
            lax.fori_loop(0, VECS, regroup, 0)
        message(k, 2).wait_recv()
        message(k, 3).wait_recv()
        finish_t(k)

        def halo():
            z_forward(k + 1, 1)
            z_backward(k + 1, 1)
            message(k, 0).wait_recv()
            message(k, 1).wait_recv()
            finish_z(k)
        local(k + 1, 1, halo)
        z_forward(k + 1, 0)
        z_forward(k + 1, 2)
        z_backward(k + 1, 0)
        z_backward(k + 1, 2)
        for i in range(4):
            corner(p, i).wait_recv()
        if p == 0:
            for i in range(4):
                corner_link(i).wait_recv()
            for i, to in enumerate((2, 6, 8 + 4, 8 + 6, 3, 1, 8 + 5, 8 + 1)):
                rl[pl.ds(24 * to, 24), :] = ll[i]
        correct(p)
        message(k + 1, 2).wait_recv()
        message(k + 1, 3).wait_recv()
        correct_t(k + 1)
        finish_t(k + 1)
        if p == 1:
            for h in range(2):
                inner[h] = products(0, h)
        message(k + 1, 0).wait_recv()
        message(k + 1, 1).wait_recv()
        correct_z(k + 1)
        finish_z(k + 1)

    pooled = []
    i0 = lax.broadcasted_iota(jnp.int32, (VECS * 16, 256), 0) & 15
    i1 = lax.broadcasted_iota(jnp.int32, (VECS * 16, 256), 1) & 15
    for h in range(2):
        prod = jnp.where(i0 == i1, inner[h] + products(1, h), 0.0)
        pooled.append(jnp.sum(prod.reshape(VECS, 16, 256), axis=1))
    zero = jnp.zeros((2 * VECS, 128), F32)
    pooled = jnp.concatenate(pooled, axis=0)
    first = jnp.concatenate([pooled[:, :128], zero], axis=1)
    second = jnp.concatenate([zero, pooled[:, 128:]], axis=1)
    values = jnp.concatenate([first, second, jnp.zeros((32, 256), F32)], axis=0)
    so[...] = lax.dot_general(
        place[...], values, (((1,), (1,)), ((), ())), preferred_element_type=F32,
        precision=lax.Precision.HIGHEST,
    )

    def exchange(d):
        to = lax.rem(me_t + d, TA)
        return pltpu.make_async_remote_copy(
            src_ref=so.at[pl.ds(pl.multiple_of(8 * to, 8), 8)],
            dst_ref=rc.at[pl.ds(pl.multiple_of(8 * me_t, 8), 8)],
            send_sem=all_send.at[d], recv_sem=all_recv.at[d],
            device_id=(me_z, to), device_id_type=MESH,
        )

    for d in FAR_FIRST:
        exchange(d).start()
    mine = pl.ds(pl.multiple_of(8 * me_t, 8), 8)
    rc[mine, :] = so[mine, :]

    def solution_rows(i, carry):
        at = [pl.ds(pl.multiple_of(n * FIELD + i * 32, 8), 32) for n in range(4)]
        total = y[at[2], :] + HALF * y[at[3], :]
        total = y[at[1], :] + HALF * total
        total = y[at[0], :] + HALF * total
        x_out[at[0], :] = WEIGHT * total
        return carry
    lax.fori_loop(0, COMPS, solution_rows, 0)

    for d in range(1, TA):
        exchange(d).wait()
    for r in range(2):
        coarse_out[pl.ds(r, TA, stride=2), :] = rc[pl.ds(r, TA, stride=8), :]
    for p in range(2):
        for m in range(4):
            message(2 * p, m).wait_send()
            message(2 * p + 1, m).wait_send()
        for i in range(4):
            corner(p, i).wait_send()
    for i in range(4):
        corner_link(i).wait_send()


def keep(value):
    return pltpu.with_memory_space_constraint(value, pltpu.HBM)


def on_device(source, gauge_links, clover_term, null_vectors, owners):
    hbm = pl.BlockSpec(memory_space=pltpu.HBM)
    vmem = pl.BlockSpec(memory_space=pltpu.VMEM)
    dma = pltpu.SemaphoreType.DMA
    x, coarse = pl.pallas_call(
        kernel,
        out_shape=(pltpu.VMEM((FIELD, 128), F32), pltpu.VMEM((2 * TA, 128), F32)),
        in_specs=[hbm] * 5,
        out_specs=(vmem, vmem),
        scratch_shapes=[
            pltpu.VMEM((5 * FIELD, 128), F32),
            pltpu.VMEM((72 * PLANE, 128), F32),
            pltpu.VMEM((144 * PLANE, 128), F32),
            pltpu.VMEM((VECS, FIELD, 128), BF16),
            pltpu.VMEM((4, 2, 96, 128), F32),
            pltpu.VMEM((4, 2, 48, 128), F32),
            pltpu.VMEM((2, 4, 24, 128), F32),
            pltpu.VMEM((6, 24, 128), F32),
            pltpu.VMEM((8, 24, 128), F32),
            pltpu.VMEM((4, 2, 96, 128), F32),
            pltpu.VMEM((4, 2, 48, 128), F32),
            pltpu.VMEM((2, 96, 128), F32),
            pltpu.VMEM((16 * 24, 128), F32),
            pltpu.VMEM((96, 128), F32),
            pltpu.VMEM((4, 256, 1536), BF16),
            pltpu.VMEM((2, VECS * 16, 256), F32),
            pltpu.VMEM((128, 256), F32),
            pltpu.VMEM((128, 128), F32),
            pltpu.VMEM((128, 128), F32),
            pltpu.VMEM((1, 16), jnp.int32),
            dma((6,)), dma((4, 4)), dma((4, 4)), dma((2, 4)), dma((2, 4)),
            dma((4,)), dma((4,)), dma((TA,)), dma((TA,)),
        ],
        compiler_params=pltpu.CompilerParams(
            collective_id=0, has_side_effects=True, vmem_limit_bytes=40 * 1024 * 1024
        ),
    )(
        keep(source.reshape(FIELD, 128)),
        keep(gauge_links.reshape(72 * PLANE, 128)),
        keep(clover_term.reshape(144 * PLANE, 128)),
        keep(null_vectors.reshape(VECS, FIELD, 128)),
        keep(owners.reshape(1, 16)),
    )
    return x.reshape(source.shape), coarse[:, :4 * VECS].T


def solution(mesh):
    in_specs = (
        P(None, "gz", "ta", None),
        P(None, None, "gz", "ta", None),
        P(None, None, None, None, "gz", "ta", None),
        P(None, None, "gz", "ta", None),
        P(("gz", "ta"), None),
    )
    out_specs = (P(None, "gz", "ta", None), P(None, ("gz", "ta")))
    return jax.shard_map(
        on_device, mesh=mesh, in_specs=in_specs, out_specs=out_specs, check_vma=False
    )
```

```python
import jax
import jax.numpy as jnp
from jax import lax
from jax.experimental import pallas as pl
from jax.experimental.pallas import tpu as pltpu
from jax.sharding import PartitionSpec as P

MESH = pl.DeviceIdType.MESH
F32 = jnp.float32
BF16 = jnp.bfloat16

NZ = 4
COMPS = 24
VECS = 24
GZ = 8
TA = 16
PLANE = 32
FIELD = COMPS * PLANE
WEIGHT = 0.24
MASS = 4.2
HALF = 0.5 * WEIGHT
KAPPA = 2.0 / WEIGHT - 2.0 * MASS
X, Y, Z, T = 0, 1, 2, 3

SPIN = {
    X: [[(-1, 1, 1), (-1, 1, 0)], [(1, 0, 1), (1, 0, 0)]],
    Y: [[(1, 0, 1), (-1, 0, 0)], [(1, 1, 1), (-1, 1, 0)]],
    Z: [[(-1, 1, 0), (1, 1, 1)], [(1, 0, 0), (-1, 0, 1)]],
    T: [[(-1, 0, 0), (-1, 0, 1)], [(-1, 1, 0), (-1, 1, 1)]],
}
CORNERS = ((-1, 1), (-1, -1), (1, 1), (1, -1))
INVERSE = {X: -1, Y: -1, Z: -1, T: 1}


LINK_ROWS = ((0, (0,)), (24, (1, 2, 3)), (80, (2,)), (104, (3, 0, 1)))
NEAR_FIRST = (1, 15, 2, 14, 3, 13, 4, 12, 5, 11, 6, 10, 7, 9, 8)
FAR_FIRST = (8, 7, 9, 6, 10, 5, 11, 4, 12, 3, 13, 2, 14, 1, 15)


def comp(reim, spin, colour):
    return 12 * reim + 3 * spin + colour


def half(reim, spin, colour):
    return 6 * reim + 3 * spin + colour


def add(a, b, sign):
    return a + b if sign > 0 else a - b


def project(load, direction, parity, s):
    out = []
    for r in range(2):
        sign, r2, s2 = SPIN[direction][r][s]
        out.append([add(load(r, s, c), load(r2, 2 + s2, c), -parity * sign) for c in range(3)])
    return out


def colour(link, a, dagger):
    re, im = [], []
    for row in range(3):
        tr = ti = None
        for k in range(3):
            e = 3 * k + row if dagger else 3 * row + k
            lr, li = link[e], link[9 + e]
            if dagger:
                nr = lr * a[0][k] + li * a[1][k]
                ni = lr * a[1][k] - li * a[0][k]
            else:
                nr = lr * a[0][k] - li * a[1][k]
                ni = lr * a[1][k] + li * a[0][k]
            tr = nr if tr is None else tr + nr
            ti = ni if ti is None else ti + ni
        re.append(tr)
        im.append(ti)
    return [re, im]


def lower_terms(direction, s):
    out = []
    for r in range(2):
        for spin in range(2):
            sign, r2, s2 = SPIN[direction][r][spin]
            if s2 == s:
                out.append((INVERSE[direction] * sign, r2, r, 2 + spin))
    return out


def kernel(
    source, links, clover, vectors, owners, x_out, coarse_out,
    y, g, cl, v, sz, st, sr, sl, ll, rz, rt, rd, rl, tmp, wt, inner, place, so, rc, ow,
    load_sem, msg_send, msg_recv, diag_send, diag_recv, link_send, link_recv, all_send, all_recv,
):
    me_z = lax.axis_index("gz")
    me_t = lax.axis_index("ta")

    def device(dz, dt):
        return (lax.rem(me_z + (dz + GZ), GZ), lax.rem(me_t + (dt + TA), TA))

    def prepare():
        loads[5].wait()
        sub = lax.broadcasted_iota(jnp.int32, (16, 128), 0)
        lane = lax.broadcasted_iota(jnp.int32, (16, 128), 1)
        padded = jnp.concatenate([ow[...].astype(F32), jnp.full((1, 112), -1.0, F32)], axis=1)
        own_row = jnp.broadcast_to(padded, (16, 128))
        own = jnp.sum(jnp.where(sub == lane, own_row, 0.0), axis=1, keepdims=True)
        rank = jnp.sum(jnp.where((own == own_row) & (lane < sub), 1.0, 0.0), axis=1, keepdims=True)
        slot = own * 8.0 + rank
        for part in range(2):
            agg = ((lane & 7) >> 2) * 8 + ((lane >> 4) & 7)
            of_lane = jnp.sum(jnp.where(agg == sub, slot, 0.0), axis=0, keepdims=True)
            row = lax.broadcasted_iota(jnp.int32, (128, 128), 0).astype(F32)
            ones = jnp.where(row == of_lane, 1.0, 0.0).astype(BF16)
            for copy in range(3):
                place[:, 256 * copy + 128 * part:256 * copy + 128 * (part + 1)] = ones

        for j in range(16):
            for e in (0, 8, 16):
                diag = lax.broadcasted_iota(jnp.int32, (8, 128), 0) + e
                rl[pl.ds(24 * j + e, 8), :] = jnp.where(
                    (diag == 0) | (diag == 4) | (diag == 8), jnp.ones((8, 128), F32), 0.0
                )

    half_links = 36 * PLANE
    loads = [
        pltpu.make_async_copy(source, y.at[pl.ds(0, FIELD)], load_sem.at[0]),
        pltpu.make_async_copy(links.at[pl.ds(half_links, half_links)], g.at[pl.ds(half_links, half_links)], load_sem.at[1]),
        pltpu.make_async_copy(links.at[pl.ds(0, half_links)], g.at[pl.ds(0, half_links)], load_sem.at[2]),
        pltpu.make_async_copy(clover, cl, load_sem.at[3]),
        pltpu.make_async_copy(vectors, v, load_sem.at[4]),
        pltpu.make_async_copy(owners, ow, load_sem.at[5]),
    ]
    for c in loads[:4] + loads[5:]:
        c.start()

    barrier = pltpu.get_barrier_semaphore()
    greet = [(dz, dt) for dz in (-1, 1) for dt in (0, -1, 1)] + [(0, dt) for dt in NEAR_FIRST]
    for dz, dt in greet:
        pl.semaphore_signal(barrier, inc=1, device_id=device(dz, dt), device_id_type=MESH)

    down_sign = jnp.where(me_t == 0, -1.0, 1.0).astype(F32)
    up_sign = jnp.where(me_t == TA - 1, -1.0, 1.0).astype(F32)

    def yrow(k, c, z, t=0):
        return k * FIELD + c * PLANE + z * 8 + t

    def y_at(k, z):
        def load(r, s, c):
            return y[pl.ds(pl.multiple_of(yrow(k, comp(r, s, c), z), 8), 8), :]
        return load

    def link_at(direction, z):
        return [
            g[pl.ds(pl.multiple_of((18 * direction + e) * PLANE + z * 8, 8), 8), :]
            for e in range(18)
        ]

    def bump(k, z, r, s, c, value, sign=1):
        at = pl.ds(pl.multiple_of(yrow(k, comp(r, s, c), z), 8), 8)
        y[at, :] = add(y[at, :], value, sign)

    y_lane = lax.broadcasted_iota(jnp.int32, (8, 128), 1) & 15
    t_row = lax.broadcasted_iota(jnp.int32, (8, 128), 0)

    def ahead(direction, a):
        if direction == X:
            return pltpu.roll(a, 112, 1)
        if direction == Y:
            return jnp.where(y_lane == 15, pltpu.roll(a, 15, 1), pltpu.roll(a, 127, 1))
        return jnp.where(t_row == 7, 0.0, pltpu.roll(a, 7, 0))

    def behind(direction, a):
        if direction == X:
            return pltpu.roll(a, 16, 1)
        if direction == Y:
            return jnp.where(y_lane == 0, pltpu.roll(a, 113, 1), pltpu.roll(a, 1, 1))
        return jnp.where(t_row == 0, 0.0, pltpu.roll(a, 1, 0))

    def layer(k, z):
        load = y_at(k, z)
        for h in range(2):
            vr = [load(0, 2 * h + i // 3, i % 3) for i in range(6)]
            vi = [load(1, 2 * h + i // 3, i % 3) for i in range(6)]
            ur = [-2.0 * a for a in vr]
            ui = [-2.0 * a for a in vi]
            for row in range(6):
                tr = KAPPA * vr[row]
                ti = KAPPA * vi[row]
                for k2 in range(6):
                    base = ((2 * h) * 6 + row) * 6 + k2
                    cr = cl[pl.ds(pl.multiple_of(base * PLANE + z * 8, 8), 8), :]
                    ci = cl[pl.ds(pl.multiple_of((base + 36) * PLANE + z * 8, 8), 8), :]
                    tr = tr + (cr * ur[k2] - ci * ui[k2])
                    ti = ti + (cr * ui[k2] + ci * ur[k2])
                s, c = 2 * h + row // 3, row % 3
                y[pl.ds(pl.multiple_of(yrow(k + 1, comp(0, s, c), z), 8), 8), :] = tr
                y[pl.ds(pl.multiple_of(yrow(k + 1, comp(1, s, c), z), 8), 8), :] = ti
        for direction in (X, Y, T):
            link = link_at(direction, z)
            for s in range(2):
                fwd = project(load, direction, -1, s)
                fwd = [[ahead(direction, a) for a in part] for part in fwd]
                fwd = colour(link, fwd, False)
                bwd = colour(link, project(load, direction, 1, s), True)
                bwd = [[behind(direction, a) for a in part] for part in bwd]
                for r in range(2):
                    for c in range(3):
                        bump(k + 1, z, r, s, c, fwd[r][c] + bwd[r][c])
                for sign, r2, r, s2 in lower_terms(direction, s):
                    for c in range(3):
                        bump(k + 1, z, r, s2, c, fwd[r2][c] - bwd[r2][c], sign)

    def z_forward(k, z):
        link = link_at(Z, z)
        for s in range(2):
            put_half(k + 1, z, s, colour(link, project(y_at(k, z + 1), Z, -1, s), False), 1)

    def z_backward(k, z):
        link = link_at(Z, z)
        for s in range(2):
            put_half(k + 1, z + 1, s, colour(link, project(y_at(k, z), Z, 1, s), True), -1)

    def put_half(k, z, s, w, parity):
        for r in range(2):
            for c in range(3):
                bump(k, z, r, s, c, w[r][c])
        for sign, r2, r, s2 in lower_terms(Z, s):
            for c in range(3):
                bump(k, z, r, s2, c, w[r2][c], parity * sign)

    def local(k, first, at_third):
        def step(i, carry):
            @pl.when(i == 2)
            def _():
                at_third()
            layer(k, lax.rem(i + first, NZ))
            return carry
        lax.fori_loop(0, NZ, step, 0)

    def rows_of(k, t):
        def load(r, s, c):
            return y[pl.ds(yrow(k, comp(r, s, c), 0, t), NZ, stride=8), :]
        return load

    def link_rows(t):
        return [g[pl.ds((18 * T + e) * PLANE + t, NZ, stride=8), :] for e in range(18)]

    def pack_z(k):
        link = link_at(Z, NZ - 1)
        for s in range(2):
            dn = project(y_at(k, 0), Z, -1, s)
            up = colour(link, project(y_at(k, NZ - 1), Z, 1, s), True)
            for r in range(2):
                for c in range(3):
                    sz[k, 0, pl.ds(8 * half(r, s, c), 8), :] = dn[r][c]
                    sz[k, 1, pl.ds(8 * half(r, s, c), 8), :] = up[r][c]
        message(k, 0).start()
        message(k, 1).start()

    def pack_t(k):
        tlink = link_rows(7)
        for s in range(2):
            dn = project(rows_of(k, 0), T, -1, s)
            up = colour(tlink, project(rows_of(k, 7), T, 1, s), True)
            for r in range(2):
                for c in range(3):
                    at = pl.ds(half(r, s, c), NZ, stride=12)
                    st[k, 0, at, :] = dn[r][c] * down_sign
                    st[k, 1, at, :] = up[r][c] * up_sign
        message(k, 2).start()
        message(k, 3).start()

    def pack_corners(p, k):
        for i, (dz, dt) in enumerate(CORNERS):
            m = 1 if dt > 0 else 0
            z = NZ - 1 if dz > 0 else 0
            sr[p, i, pl.ds(0, 12), :] = st[k, m, pl.ds(12 * z, 12), :]
            t, sign = (7, up_sign) if dt > 0 else (0, down_sign)
            sr[p, i, pl.ds(12, 12), :] = sz[k, 1 if dz > 0 else 0, pl.ds(t, 12, stride=8), :] * sign
            corner(p, i).start()

    def message(k, m):
        target = ((-1, 0), (1, 0), (0, -1), (0, 1))[m]
        src, dst = (sz, rz) if m < 2 else (st, rt)
        return pltpu.make_async_remote_copy(
            src_ref=src.at[k, m % 2], dst_ref=dst.at[k, m % 2],
            send_sem=msg_send.at[k, m], recv_sem=msg_recv.at[k, m],
            device_id=device(*target), device_id_type=MESH,
        )

    def corner(p, i):
        return pltpu.make_async_remote_copy(
            src_ref=sr.at[p, i], dst_ref=rd.at[p, pl.ds(24 * i, 24)],
            send_sem=diag_send.at[p, i], recv_sem=diag_recv.at[p, i],
            device_id=device(*CORNERS[i]), device_id_type=MESH,
        )

    def corner_link(i):
        target = ((-1, 0), (1, 0), (0, -1), (0, 1))[i]
        at = pl.ds(LINK_ROWS[i][0], 24 if len(LINK_ROWS[i][1]) == 1 else 56)
        return pltpu.make_async_remote_copy(
            src_ref=sl.at[at], dst_ref=ll.at[at],
            send_sem=link_send.at[i], recv_sem=link_recv.at[i],
            device_id=device(*target), device_id_type=MESH,
        )

    def finish_t(k):
        link = link_rows(7)
        for s in range(2):
            a = [[rt[k, 0, pl.ds(half(r, s, c), NZ, stride=12), :] for c in range(3)] for r in range(2)]
            b = [[rt[k, 1, pl.ds(half(r, s, c), NZ, stride=12), :] for c in range(3)] for r in range(2)]
            for w, t, parity in ((colour(link, a, False), 7, 1), (b, 0, -1)):
                def bump_row(r, s, c, value, sign):
                    at = pl.ds(yrow(k + 1, comp(r, s, c), 0, t), NZ, stride=8)
                    y[at, :] = add(y[at, :], value, sign)
                for r in range(2):
                    for c in range(3):
                        bump_row(r, s, c, w[r][c], 1)
                for sign, r2, r, s2 in lower_terms(T, s):
                    for c in range(3):
                        bump_row(r, s2, c, w[r2][c], parity * sign)

    def finish_z(k):
        link = link_at(Z, NZ - 1)
        for s in range(2):
            a = [[rz[k, 0, pl.ds(8 * half(r, s, c), 8), :] for c in range(3)] for r in range(2)]
            put_half(k + 1, NZ - 1, s, colour(link, a, False), 1)
            b = [[rz[k, 1, pl.ds(8 * half(r, s, c), 8), :] for c in range(3)] for r in range(2)]
            put_half(k + 1, 0, s, b, -1)

    def correct(p):
        one = [rl[pl.ds(e, 8, stride=24), :] for e in range(18)]
        two = [rl[pl.ds(192 + e, 8, stride=24), :] for e in range(18)]
        j = lax.broadcasted_iota(jnp.int32, (8, 128), 0)
        plus = (j == 0) | (j == 3) | (j == 5) | (j == 6)
        sign_j = jnp.where(plus, jnp.ones((8, 128), F32), -1.0)
        w = []
        for s in range(2):
            a = [[rd[p, pl.ds(half(r, s, c), 8, stride=12), :] for c in range(3)] for r in range(2)]
            w.append(colour(one, a, False))
        for s in range(2):
            q = []
            for r in range(2):
                sign, r2, s2 = SPIN[Z][r][s]
                q.append([add(w[s][r][c], sign_j * w[s2][r2][c], sign) for c in range(3)])
            q = colour(two, q, True)
            for r in range(2):
                for c in range(3):
                    tmp[pl.ds(8 * half(r, s, c), 8), :] = q[r][c]

    def correct_z(k):
        for n in range(12):
            for m in range(2):
                at = pl.ds(8 * n, 2, stride=7)
                rz[k, m, at, :] = rz[k, m, at, :] + tmp[pl.ds(8 * n + 4 * m, 2, stride=2), :]

    def correct_t(k):
        for n in range(12):
            for m, z, pos in ((0, 0, 7), (0, 3, 3), (1, 0, 5), (1, 3, 1)):
                at = pl.ds(12 * z + n, 1)
                rt[k, m, at, :] = rt[k, m, at, :] + tmp[pl.ds(8 * n + pos, 1), :]

    def regroup(n, carry):
        for c in range(COMPS):
            f = v[n, pl.ds(c * PLANE, PLANE), :].astype(F32)
            v[n, pl.ds(c * PLANE, PLANE), :] = jnp.concatenate([f[8:24], f[:8], f[24:]], axis=0).astype(BF16)
        return carry

    def products(part, h):
        site = lax.broadcasted_iota(jnp.int32, (16, 128), 1)
        group = (site >> 6) * 4 + ((site & 15) >> 2)
        scale = HALF ** 4
        left = []
        for c in range(6):
            rows = []
            for r in range(2):
                n = comp(r, 2 * h, 0) + c
                if part == 0:
                    field = y[pl.ds(yrow(4, n, 1), 16), :]
                else:
                    field = jnp.concatenate([y[pl.ds(yrow(4, n, 0), 8), :], y[pl.ds(yrow(4, n, 3), 8), :]], axis=0)
                rows.append((field * scale).astype(BF16))
                left.append(v[:, pl.ds(n * PLANE + 16 * part, 16), :].reshape(VECS * 16, 128))
            for grp in range(8):
                keep = (group == grp).astype(F32).astype(BF16)
                re, im = rows[0] * keep, rows[1] * keep
                col = 256 * c
                wt[2 * part + h, pl.ds(16 * grp, 16), col:col + 128] = re
                wt[2 * part + h, pl.ds(16 * grp, 16), col + 128:col + 256] = im
                wt[2 * part + h, pl.ds(128 + 16 * grp, 16), col:col + 128] = im
                wt[2 * part + h, pl.ds(128 + 16 * grp, 16), col + 128:col + 256] = -re
        return lax.dot_general(
            jnp.concatenate(left, axis=1), wt[2 * part + h], (((1,), (1,)), ((), ())), preferred_element_type=F32
        )

    loads[0].wait()
    loads[1].wait()
    pl.semaphore_wait(barrier, len(greet))

    for p in range(2):
        k = 2 * p
        pack_z(k)
        pack_t(k)
        pack_corners(p, k)
        if p == 0:
            corner_rows = ((T, 0, 7), (T, 3, 7), (Z, 3, 0), (Z, 3, 7))
            for base, blocks in LINK_ROWS:
                for n, b in enumerate(blocks):
                    direction, z, t = corner_rows[b]
                    rows = g[pl.ds((18 * direction) * PLANE + z * 8 + t, 18, stride=32), :]
                    sl[pl.ds(base + 18 * n, 18), :] = rows
            for i in range(4):
                corner_link(i).start()
            loads[2].wait()
            loads[3].wait()
            loads[4].start()

        def faces():
            z_backward(k, NZ - 2)
            z_forward(k, 0)
            pack_z(k + 1)
        local(k, NZ - 1, faces)
        z_forward(k, 1)
        z_forward(k, 2)
        z_backward(k, 0)
        z_backward(k, 1)
        pack_t(k + 1)
        if p == 0:
            prepare()
            loads[4].wait()
            lax.fori_loop(0, VECS, regroup, 0)
        message(k, 2).wait_recv()
        message(k, 3).wait_recv()
        finish_t(k)

        def halo():
            z_forward(k + 1, 1)
            z_backward(k + 1, 1)
            message(k, 0).wait_recv()
            message(k, 1).wait_recv()
            finish_z(k)
        local(k + 1, 1, halo)
        z_forward(k + 1, 0)
        z_forward(k + 1, 2)
        z_backward(k + 1, 0)
        z_backward(k + 1, 2)
        for i in range(4):
            corner(p, i).wait_recv()
        if p == 0:
            for i in range(4):
                corner_link(i).wait_recv()
            for (base, _), slots in zip(LINK_ROWS, ((2,), (6, 12, 14), (3,), (1, 13, 9))):
                for n, to in enumerate(slots):
                    rl[pl.ds(24 * to, 18), :] = ll[pl.ds(base + 18 * n, 18), :]
        correct(p)
        message(k + 1, 2).wait_recv()
        message(k + 1, 3).wait_recv()
        correct_t(k + 1)
        finish_t(k + 1)
        if p == 1:
            for h in range(2):
                inner[h] = products(0, h)
        message(k + 1, 0).wait_recv()
        message(k + 1, 1).wait_recv()
        correct_z(k + 1)
        finish_z(k + 1)

    pooled = []
    i0 = lax.broadcasted_iota(jnp.int32, (VECS * 16, 256), 0) & 15
    i1 = lax.broadcasted_iota(jnp.int32, (VECS * 16, 256), 1) & 15
    for h in range(2):
        prod = jnp.where(i0 == i1, inner[h] + products(1, h), 0.0)
        pooled.append(jnp.sum(prod.reshape(VECS, 16, 256), axis=1))
    zero = jnp.zeros((2 * VECS, 128), F32)
    pooled = jnp.concatenate(pooled, axis=0)
    first = jnp.concatenate([pooled[:, :128], zero], axis=1)
    second = jnp.concatenate([zero, pooled[:, 128:]], axis=1)
    values = jnp.concatenate([first, second, jnp.zeros((32, 256), F32)], axis=0)
    high = values.astype(BF16)
    rest = values - high.astype(F32)
    middle = rest.astype(BF16)
    low = (rest - middle.astype(F32)).astype(BF16)
    so[...] = lax.dot_general(
        place[...], jnp.concatenate([high, middle, low], axis=1), (((1,), (1,)), ((), ())),
        preferred_element_type=F32,
    )

    def exchange(d):
        to = lax.rem(me_t + d, TA)
        return pltpu.make_async_remote_copy(
            src_ref=so.at[pl.ds(pl.multiple_of(8 * to, 8), 8)],
            dst_ref=rc.at[pl.ds(pl.multiple_of(8 * me_t, 8), 8)],
            send_sem=all_send.at[d], recv_sem=all_recv.at[d],
            device_id=(me_z, to), device_id_type=MESH,
        )

    for d in FAR_FIRST:
        exchange(d).start()
    mine = pl.ds(pl.multiple_of(8 * me_t, 8), 8)
    rc[mine, :] = so[mine, :]

    def solution_rows(i, carry):
        at = [pl.ds(pl.multiple_of(n * FIELD + i * 32, 8), 32) for n in range(4)]
        total = y[at[2], :] + HALF * y[at[3], :]
        total = y[at[1], :] + HALF * total
        total = y[at[0], :] + HALF * total
        x_out[at[0], :] = WEIGHT * total
        return carry
    lax.fori_loop(0, COMPS, solution_rows, 0)

    for d in range(1, TA):
        exchange(d).wait()
    for r in range(2):
        coarse_out[pl.ds(r, TA, stride=2), :] = rc[pl.ds(r, TA, stride=8), :]
    for p in range(2):
        for m in range(4):
            message(2 * p, m).wait_send()
            message(2 * p + 1, m).wait_send()
        for i in range(4):
            corner(p, i).wait_send()
    for i in range(4):
        corner_link(i).wait_send()


def keep(value):
    return pltpu.with_memory_space_constraint(value, pltpu.HBM)


def on_device(source, gauge_links, clover_term, null_vectors, owners):
    hbm = pl.BlockSpec(memory_space=pltpu.HBM)
    vmem = pl.BlockSpec(memory_space=pltpu.VMEM)
    dma = pltpu.SemaphoreType.DMA
    x, coarse = pl.pallas_call(
        kernel,
        out_shape=(pltpu.VMEM((FIELD, 128), F32), pltpu.VMEM((2 * TA, 128), F32)),
        in_specs=[hbm] * 5,
        out_specs=(vmem, vmem),
        scratch_shapes=[
            pltpu.VMEM((5 * FIELD, 128), F32),
            pltpu.VMEM((72 * PLANE, 128), F32),
            pltpu.VMEM((144 * PLANE, 128), F32),
            pltpu.VMEM((VECS, FIELD, 128), BF16),
            pltpu.VMEM((4, 2, 96, 128), F32),
            pltpu.VMEM((4, 2, 48, 128), F32),
            pltpu.VMEM((2, 4, 24, 128), F32),
            pltpu.VMEM((160, 128), F32),
            pltpu.VMEM((160, 128), F32),
            pltpu.VMEM((4, 2, 96, 128), F32),
            pltpu.VMEM((4, 2, 48, 128), F32),
            pltpu.VMEM((2, 96, 128), F32),
            pltpu.VMEM((16 * 24, 128), F32),
            pltpu.VMEM((96, 128), F32),
            pltpu.VMEM((4, 256, 1536), BF16),
            pltpu.VMEM((2, VECS * 16, 256), F32),
            pltpu.VMEM((128, 768), BF16),
            pltpu.VMEM((128, 128), F32),
            pltpu.VMEM((128, 128), F32),
            pltpu.VMEM((1, 16), jnp.int32),
            dma((6,)), dma((4, 4)), dma((4, 4)), dma((2, 4)), dma((2, 4)),
            dma((4,)), dma((4,)), dma((TA,)), dma((TA,)),
        ],
        compiler_params=pltpu.CompilerParams(
            collective_id=0, has_side_effects=True, vmem_limit_bytes=40 * 1024 * 1024
        ),
    )(
        keep(source.reshape(FIELD, 128)),
        keep(gauge_links.reshape(72 * PLANE, 128)),
        keep(clover_term.reshape(144 * PLANE, 128)),
        keep(null_vectors.reshape(VECS, FIELD, 128)),
        keep(owners.reshape(1, 16)),
    )
    return x.reshape(source.shape), coarse[:, :4 * VECS].T


def solution(mesh):
    in_specs = (
        P(None, "gz", "ta", None),
        P(None, None, "gz", "ta", None),
        P(None, None, None, None, "gz", "ta", None),
        P(None, None, "gz", "ta", None),
        P(("gz", "ta"), None),
    )
    out_specs = (P(None, "gz", "ta", None), P(None, ("gz", "ta")))
    return jax.shard_map(
        on_device, mesh=mesh, in_specs=in_specs, out_specs=out_specs, check_vma=False
    )
```

```python
import jax
import jax.numpy as jnp
from jax import lax
from jax.experimental import pallas as pl
from jax.experimental.pallas import tpu as pltpu
from jax.sharding import PartitionSpec as P

MESH = pl.DeviceIdType.MESH
F32 = jnp.float32
BF16 = jnp.bfloat16

NZ = 4
COMPS = 24
VECS = 24
GZ = 8
TA = 16
PLANE = 32
FIELD = COMPS * PLANE
WEIGHT = 0.24
MASS = 4.2
HALF = 0.5 * WEIGHT
KAPPA = 2.0 / WEIGHT - 2.0 * MASS
X, Y, Z, T = 0, 1, 2, 3

SPIN = {
    X: [[(-1, 1, 1), (-1, 1, 0)], [(1, 0, 1), (1, 0, 0)]],
    Y: [[(1, 0, 1), (-1, 0, 0)], [(1, 1, 1), (-1, 1, 0)]],
    Z: [[(-1, 1, 0), (1, 1, 1)], [(1, 0, 0), (-1, 0, 1)]],
    T: [[(-1, 0, 0), (-1, 0, 1)], [(-1, 1, 0), (-1, 1, 1)]],
}
CORNERS = ((-1, 1), (-1, -1), (1, 1), (1, -1))
INVERSE = {X: -1, Y: -1, Z: -1, T: 1}


LINK_ROWS = ((0, (0,)), (24, (1, 2, 3)), (80, (2,)), (104, (3, 0, 1)))
NEAR_FIRST = (1, 15, 2, 14, 3, 13, 4, 12, 5, 11, 6, 10, 7, 9, 8)
FAR_FIRST = (8, 7, 9, 6, 10, 5, 11, 4, 12, 3, 13, 2, 14, 1, 15)


def comp(reim, spin, colour):
    return 12 * reim + 3 * spin + colour


def half(reim, spin, colour):
    return 6 * reim + 3 * spin + colour


def add(a, b, sign):
    return a + b if sign > 0 else a - b


def project(load, direction, parity, s):
    out = []
    for r in range(2):
        sign, r2, s2 = SPIN[direction][r][s]
        out.append([add(load(r, s, c), load(r2, 2 + s2, c), -parity * sign) for c in range(3)])
    return out


def colour(link, a, dagger):
    re, im = [], []
    for row in range(3):
        tr = ti = None
        for k in range(3):
            e = 3 * k + row if dagger else 3 * row + k
            lr, li = link[e], link[9 + e]
            if dagger:
                nr = lr * a[0][k] + li * a[1][k]
                ni = lr * a[1][k] - li * a[0][k]
            else:
                nr = lr * a[0][k] - li * a[1][k]
                ni = lr * a[1][k] + li * a[0][k]
            tr = nr if tr is None else tr + nr
            ti = ni if ti is None else ti + ni
        re.append(tr)
        im.append(ti)
    return [re, im]


def lower_terms(direction, s):
    out = []
    for r in range(2):
        for spin in range(2):
            sign, r2, s2 = SPIN[direction][r][spin]
            if s2 == s:
                out.append((INVERSE[direction] * sign, r2, r, 2 + spin))
    return out


def kernel(
    source, links, clover, vectors, owners, x_out, coarse_out,
    y, g, cl, v, sz, st, sr, sl, ll, rz, rt, rd, rl, tmp, wt, inner, place, so, rc, ow,
    load_sem, msg_send, msg_recv, diag_send, diag_recv, link_send, link_recv, all_send, all_recv,
):
    me_z = lax.axis_index("gz")
    me_t = lax.axis_index("ta")

    def device(dz, dt):
        return (lax.rem(me_z + (dz + GZ), GZ), lax.rem(me_t + (dt + TA), TA))

    def prepare():
        loads[5].wait()
        sub = lax.broadcasted_iota(jnp.int32, (16, 128), 0)
        lane = lax.broadcasted_iota(jnp.int32, (16, 128), 1)
        padded = jnp.concatenate([ow[...].astype(F32), jnp.full((1, 112), -1.0, F32)], axis=1)
        own_row = jnp.broadcast_to(padded, (16, 128))
        own = jnp.sum(jnp.where(sub == lane, own_row, 0.0), axis=1, keepdims=True)
        rank = jnp.sum(jnp.where((own == own_row) & (lane < sub), 1.0, 0.0), axis=1, keepdims=True)
        slot = own * 8.0 + rank
        for part in range(2):
            agg = ((lane & 7) >> 2) * 8 + ((lane >> 4) & 7)
            of_lane = jnp.sum(jnp.where(agg == sub, slot, 0.0), axis=0, keepdims=True)
            row = lax.broadcasted_iota(jnp.int32, (128, 128), 0).astype(F32)
            ones = jnp.where(row == of_lane, 1.0, 0.0).astype(BF16)
            for copy in range(3):
                place[:, 256 * copy + 128 * part:256 * copy + 128 * (part + 1)] = ones

        for j in range(16):
            for e in (0, 8, 16):
                diag = lax.broadcasted_iota(jnp.int32, (8, 128), 0) + e
                rl[pl.ds(24 * j + e, 8), :] = jnp.where(
                    (diag == 0) | (diag == 4) | (diag == 8), jnp.ones((8, 128), F32), 0.0
                )

    half_links = 36 * PLANE
    loads = [
        pltpu.make_async_copy(source, y.at[pl.ds(0, FIELD)], load_sem.at[0]),
        pltpu.make_async_copy(links.at[pl.ds(half_links, half_links)], g.at[pl.ds(half_links, half_links)], load_sem.at[1]),
        pltpu.make_async_copy(links.at[pl.ds(0, half_links)], g.at[pl.ds(0, half_links)], load_sem.at[2]),
        pltpu.make_async_copy(clover, cl, load_sem.at[3]),
        pltpu.make_async_copy(vectors, v, load_sem.at[4]),
        pltpu.make_async_copy(owners, ow, load_sem.at[5]),
    ]
    for c in loads[:4] + loads[5:]:
        c.start()

    barrier = pltpu.get_barrier_semaphore()
    greet = [(dz, dt) for dz in (-1, 1) for dt in (0, -1, 1)] + [(0, dt) for dt in NEAR_FIRST]
    for dz, dt in greet:
        pl.semaphore_signal(barrier, inc=1, device_id=device(dz, dt), device_id_type=MESH)

    down_sign = jnp.where(me_t == 0, -1.0, 1.0).astype(F32)
    up_sign = jnp.where(me_t == TA - 1, -1.0, 1.0).astype(F32)

    def yrow(k, c, z, t=0):
        return k * FIELD + c * PLANE + z * 8 + t

    def y_at(k, z):
        def load(r, s, c):
            return y[pl.ds(pl.multiple_of(yrow(k, comp(r, s, c), z), 8), 8), :]
        return load

    def link_at(direction, z):
        return [
            g[pl.ds(pl.multiple_of((18 * direction + e) * PLANE + z * 8, 8), 8), :]
            for e in range(18)
        ]

    def bump(k, z, r, s, c, value, sign=1):
        at = pl.ds(pl.multiple_of(yrow(k, comp(r, s, c), z), 8), 8)
        y[at, :] = add(y[at, :], value, sign)

    y_lane = lax.broadcasted_iota(jnp.int32, (8, 128), 1) & 15
    t_row = lax.broadcasted_iota(jnp.int32, (8, 128), 0)

    def ahead(direction, a):
        if direction == X:
            return pltpu.roll(a, 112, 1)
        if direction == Y:
            return jnp.where(y_lane == 15, pltpu.roll(a, 15, 1), pltpu.roll(a, 127, 1))
        return jnp.where(t_row == 7, 0.0, pltpu.roll(a, 7, 0))

    def behind(direction, a):
        if direction == X:
            return pltpu.roll(a, 16, 1)
        if direction == Y:
            return jnp.where(y_lane == 0, pltpu.roll(a, 113, 1), pltpu.roll(a, 1, 1))
        return jnp.where(t_row == 0, 0.0, pltpu.roll(a, 1, 0))

    def layer(k, z):
        load = y_at(k, z)
        for h in range(2):
            vr = [load(0, 2 * h + i // 3, i % 3) for i in range(6)]
            vi = [load(1, 2 * h + i // 3, i % 3) for i in range(6)]
            ur = [-2.0 * a for a in vr]
            ui = [-2.0 * a for a in vi]
            for row in range(6):
                tr = KAPPA * vr[row]
                ti = KAPPA * vi[row]
                for k2 in range(6):
                    base = ((2 * h) * 6 + row) * 6 + k2
                    cr = cl[pl.ds(pl.multiple_of(base * PLANE + z * 8, 8), 8), :]
                    ci = cl[pl.ds(pl.multiple_of((base + 36) * PLANE + z * 8, 8), 8), :]
                    tr = tr + (cr * ur[k2] - ci * ui[k2])
                    ti = ti + (cr * ui[k2] + ci * ur[k2])
                s, c = 2 * h + row // 3, row % 3
                y[pl.ds(pl.multiple_of(yrow(k + 1, comp(0, s, c), z), 8), 8), :] = tr
                y[pl.ds(pl.multiple_of(yrow(k + 1, comp(1, s, c), z), 8), 8), :] = ti
        for direction in (X, Y, T):
            link = link_at(direction, z)
            for s in range(2):
                fwd = project(load, direction, -1, s)
                fwd = [[ahead(direction, a) for a in part] for part in fwd]
                fwd = colour(link, fwd, False)
                bwd = colour(link, project(load, direction, 1, s), True)
                bwd = [[behind(direction, a) for a in part] for part in bwd]
                for r in range(2):
                    for c in range(3):
                        bump(k + 1, z, r, s, c, fwd[r][c] + bwd[r][c])
                for sign, r2, r, s2 in lower_terms(direction, s):
                    for c in range(3):
                        bump(k + 1, z, r, s2, c, fwd[r2][c] - bwd[r2][c], sign)

    def z_forward(k, z):
        link = link_at(Z, z)
        for s in range(2):
            put_half(k + 1, z, s, colour(link, project(y_at(k, z + 1), Z, -1, s), False), 1)

    def z_backward(k, z):
        link = link_at(Z, z)
        for s in range(2):
            put_half(k + 1, z + 1, s, colour(link, project(y_at(k, z), Z, 1, s), True), -1)

    def put_half(k, z, s, w, parity):
        for r in range(2):
            for c in range(3):
                bump(k, z, r, s, c, w[r][c])
        for sign, r2, r, s2 in lower_terms(Z, s):
            for c in range(3):
                bump(k, z, r, s2, c, w[r2][c], parity * sign)

    def local(k, first, at_third):
        def step(i, carry):
            @pl.when(i == 2)
            def _():
                at_third()
            layer(k, lax.rem(i + first, NZ))
            return carry
        lax.fori_loop(0, NZ, step, 0)

    def rows_of(k, t):
        def load(r, s, c):
            return y[pl.ds(yrow(k, comp(r, s, c), 0, t), NZ, stride=8), :]
        return load

    def link_rows(t):
        return [g[pl.ds((18 * T + e) * PLANE + t, NZ, stride=8), :] for e in range(18)]

    def pack_z(k):
        link = link_at(Z, NZ - 1)
        for s in range(2):
            dn = project(y_at(k, 0), Z, -1, s)
            up = colour(link, project(y_at(k, NZ - 1), Z, 1, s), True)
            for r in range(2):
                for c in range(3):
                    sz[k, 0, pl.ds(8 * half(r, s, c), 8), :] = dn[r][c]
                    sz[k, 1, pl.ds(8 * half(r, s, c), 8), :] = up[r][c]
        message(k, 0).start()
        message(k, 1).start()

    def pack_t(k):
        tlink = link_rows(7)
        for s in range(2):
            dn = project(rows_of(k, 0), T, -1, s)
            up = colour(tlink, project(rows_of(k, 7), T, 1, s), True)
            for r in range(2):
                for c in range(3):
                    at = pl.ds(half(r, s, c), NZ, stride=12)
                    st[k, 0, at, :] = dn[r][c] * down_sign
                    st[k, 1, at, :] = up[r][c] * up_sign
        message(k, 2).start()
        message(k, 3).start()

    def pack_corners(p, k):
        for i, (dz, dt) in enumerate(CORNERS):
            m = 1 if dt > 0 else 0
            z = NZ - 1 if dz > 0 else 0
            sr[p, i, pl.ds(0, 12), :] = st[k, m, pl.ds(12 * z, 12), :]
            t, sign = (7, up_sign) if dt > 0 else (0, down_sign)
            sr[p, i, pl.ds(12, 12), :] = sz[k, 1 if dz > 0 else 0, pl.ds(t, 12, stride=8), :] * sign
            corner(p, i).start()

    def message(k, m):
        target = ((-1, 0), (1, 0), (0, -1), (0, 1))[m]
        src, dst = (sz, rz) if m < 2 else (st, rt)
        return pltpu.make_async_remote_copy(
            src_ref=src.at[k, m % 2], dst_ref=dst.at[k, m % 2],
            send_sem=msg_send.at[k, m], recv_sem=msg_recv.at[k, m],
            device_id=device(*target), device_id_type=MESH,
        )

    def corner(p, i):
        return pltpu.make_async_remote_copy(
            src_ref=sr.at[p, i], dst_ref=rd.at[p, pl.ds(24 * i, 24)],
            send_sem=diag_send.at[p, i], recv_sem=diag_recv.at[p, i],
            device_id=device(*CORNERS[i]), device_id_type=MESH,
        )

    def corner_link(i):
        target = ((-1, 0), (1, 0), (0, -1), (0, 1))[i]
        at = pl.ds(LINK_ROWS[i][0], 24 if len(LINK_ROWS[i][1]) == 1 else 56)
        return pltpu.make_async_remote_copy(
            src_ref=sl.at[at], dst_ref=ll.at[at],
            send_sem=link_send.at[i], recv_sem=link_recv.at[i],
            device_id=device(*target), device_id_type=MESH,
        )

    def finish_t(k):
        link = link_rows(7)
        for s in range(2):
            a = [[rt[k, 0, pl.ds(half(r, s, c), NZ, stride=12), :] for c in range(3)] for r in range(2)]
            b = [[rt[k, 1, pl.ds(half(r, s, c), NZ, stride=12), :] for c in range(3)] for r in range(2)]
            for w, t, parity in ((colour(link, a, False), 7, 1), (b, 0, -1)):
                def bump_row(r, s, c, value, sign):
                    at = pl.ds(yrow(k + 1, comp(r, s, c), 0, t), NZ, stride=8)
                    y[at, :] = add(y[at, :], value, sign)
                for r in range(2):
                    for c in range(3):
                        bump_row(r, s, c, w[r][c], 1)
                for sign, r2, r, s2 in lower_terms(T, s):
                    for c in range(3):
                        bump_row(r, s2, c, w[r2][c], parity * sign)

    def finish_z(k):
        link = link_at(Z, NZ - 1)
        for s in range(2):
            a = [[rz[k, 0, pl.ds(8 * half(r, s, c), 8), :] for c in range(3)] for r in range(2)]
            put_half(k + 1, NZ - 1, s, colour(link, a, False), 1)
            b = [[rz[k, 1, pl.ds(8 * half(r, s, c), 8), :] for c in range(3)] for r in range(2)]
            put_half(k + 1, 0, s, b, -1)

    def correct(p):
        one = [rl[pl.ds(e, 8, stride=24), :] for e in range(18)]
        two = [rl[pl.ds(192 + e, 8, stride=24), :] for e in range(18)]
        j = lax.broadcasted_iota(jnp.int32, (8, 128), 0)
        plus = (j == 0) | (j == 3) | (j == 5) | (j == 6)
        sign_j = jnp.where(plus, jnp.ones((8, 128), F32), -1.0)
        w = []
        for s in range(2):
            a = [[rd[p, pl.ds(half(r, s, c), 8, stride=12), :] for c in range(3)] for r in range(2)]
            w.append(colour(one, a, False))
        for s in range(2):
            q = []
            for r in range(2):
                sign, r2, s2 = SPIN[Z][r][s]
                q.append([add(w[s][r][c], sign_j * w[s2][r2][c], sign) for c in range(3)])
            q = colour(two, q, True)
            for r in range(2):
                for c in range(3):
                    tmp[pl.ds(8 * half(r, s, c), 8), :] = q[r][c]

    def correct_z(k):
        for n in range(12):
            for m in range(2):
                at = pl.ds(8 * n, 2, stride=7)
                rz[k, m, at, :] = rz[k, m, at, :] + tmp[pl.ds(8 * n + 4 * m, 2, stride=2), :]

    def correct_t(k):
        for n in range(12):
            for m, z, pos in ((0, 0, 7), (0, 3, 3), (1, 0, 5), (1, 3, 1)):
                at = pl.ds(12 * z + n, 1)
                rt[k, m, at, :] = rt[k, m, at, :] + tmp[pl.ds(8 * n + pos, 1), :]

    def regroup(n, carry):
        for c in range(COMPS):
            f = v[n, pl.ds(c * PLANE, PLANE), :].astype(F32)
            v[n, pl.ds(c * PLANE, PLANE), :] = jnp.concatenate([f[8:24], f[:8], f[24:]], axis=0).astype(BF16)
        return carry

    def products(part, h):
        site = lax.broadcasted_iota(jnp.int32, (16, 128), 1)
        group = (site >> 6) * 4 + ((site & 15) >> 2)
        scale = HALF ** 4
        left = []
        for c in range(6):
            rows = []
            for r in range(2):
                n = comp(r, 2 * h, 0) + c
                if part == 0:
                    field = y[pl.ds(yrow(4, n, 1), 16), :]
                else:
                    field = jnp.concatenate([y[pl.ds(yrow(4, n, 0), 8), :], y[pl.ds(yrow(4, n, 3), 8), :]], axis=0)
                rows.append((field * scale).astype(BF16))
                left.append(v[:, pl.ds(n * PLANE + 16 * part, 16), :].reshape(VECS * 16, 128))
            for grp in range(8):
                keep = (group == grp).astype(F32).astype(BF16)
                re, im = rows[0] * keep, rows[1] * keep
                col = 256 * c
                wt[2 * part + h, pl.ds(16 * grp, 16), col:col + 128] = re
                wt[2 * part + h, pl.ds(16 * grp, 16), col + 128:col + 256] = im
                wt[2 * part + h, pl.ds(128 + 16 * grp, 16), col:col + 128] = im
                wt[2 * part + h, pl.ds(128 + 16 * grp, 16), col + 128:col + 256] = -re
        return lax.dot_general(
            jnp.concatenate(left, axis=1), wt[2 * part + h], (((1,), (1,)), ((), ())), preferred_element_type=F32
        )

    loads[0].wait()
    loads[1].wait()
    pl.semaphore_wait(barrier, len(greet))

    for p in range(2):
        k = 2 * p
        pack_z(k)
        pack_t(k)
        pack_corners(p, k)
        if p == 0:
            corner_rows = ((T, 0, 7), (T, 3, 7), (Z, 3, 0), (Z, 3, 7))
            for base, blocks in LINK_ROWS:
                for n, b in enumerate(blocks):
                    direction, z, t = corner_rows[b]
                    rows = g[pl.ds((18 * direction) * PLANE + z * 8 + t, 18, stride=32), :]
                    sl[pl.ds(base + 18 * n, 18), :] = rows
            for i in range(4):
                corner_link(i).start()
            loads[2].wait()
            loads[3].wait()
            loads[4].start()

        def faces():
            z_backward(k, NZ - 2)
            z_forward(k, 0)
            pack_z(k + 1)
        local(k, NZ - 1, faces)
        z_forward(k, 1)
        z_forward(k, 2)
        z_backward(k, 0)
        z_backward(k, 1)
        pack_t(k + 1)
        if p == 0:
            prepare()
            loads[4].wait()
            lax.fori_loop(0, VECS, regroup, 0)
        message(k, 2).wait_recv()
        message(k, 3).wait_recv()
        finish_t(k)

        def halo():
            z_forward(k + 1, 1)
            z_backward(k + 1, 1)
            message(k, 0).wait_recv()
            message(k, 1).wait_recv()
            finish_z(k)
        local(k + 1, 1, halo)
        z_forward(k + 1, 0)
        z_forward(k + 1, 2)
        z_backward(k + 1, 0)
        z_backward(k + 1, 2)
        for i in range(4):
            corner(p, i).wait_recv()
        if p == 0:
            for i in range(4):
                corner_link(i).wait_recv()
            for (base, _), slots in zip(LINK_ROWS, ((2,), (6, 12, 14), (3,), (1, 13, 9))):
                for n, to in enumerate(slots):
                    rl[pl.ds(24 * to, 18), :] = ll[pl.ds(base + 18 * n, 18), :]
        correct(p)
        message(k + 1, 2).wait_recv()
        message(k + 1, 3).wait_recv()
        correct_t(k + 1)
        finish_t(k + 1)
        if p == 1:
            for h in range(2):
                inner[h] = products(0, h)
        message(k + 1, 0).wait_recv()
        message(k + 1, 1).wait_recv()
        correct_z(k + 1)
        finish_z(k + 1)

    pooled = []
    i0 = lax.broadcasted_iota(jnp.int32, (VECS * 16, 256), 0) & 15
    i1 = lax.broadcasted_iota(jnp.int32, (VECS * 16, 256), 1) & 15
    for h in range(2):
        prod = jnp.where(i0 == i1, inner[h] + products(1, h), 0.0)
        pooled.append(jnp.sum(prod.reshape(VECS, 16, 256), axis=1))
    zero = jnp.zeros((2 * VECS, 128), F32)
    pooled = jnp.concatenate(pooled, axis=0)
    first = jnp.concatenate([pooled[:, :128], zero], axis=1)
    second = jnp.concatenate([zero, pooled[:, 128:]], axis=1)
    values = jnp.concatenate([first, second, jnp.zeros((32, 256), F32)], axis=0)
    high = values.astype(BF16)
    rest = values - high.astype(F32)
    middle = rest.astype(BF16)
    low = (rest - middle.astype(F32)).astype(BF16)
    so[...] = lax.dot_general(
        place[...], jnp.concatenate([high, middle, low], axis=1), (((1,), (1,)), ((), ())),
        preferred_element_type=F32,
    )

    def exchange(d):
        to = lax.rem(me_t + d, TA)
        return pltpu.make_async_remote_copy(
            src_ref=so.at[pl.ds(pl.multiple_of(8 * to, 8), 8)],
            dst_ref=rc.at[pl.ds(pl.multiple_of(8 * me_t, 8), 8)],
            send_sem=all_send.at[d], recv_sem=all_recv.at[d],
            device_id=(me_z, to), device_id_type=MESH,
        )

    for d in FAR_FIRST:
        exchange(d).start()
    mine = pl.ds(pl.multiple_of(8 * me_t, 8), 8)
    rc[mine, :] = so[mine, :]

    def solution_rows(i, carry):
        at = [pl.ds(pl.multiple_of(n * FIELD + i * 32, 8), 32) for n in range(4)]
        total = y[at[2], :] + HALF * y[at[3], :]
        total = y[at[1], :] + HALF * total
        total = y[at[0], :] + HALF * total
        x_out[at[0], :] = WEIGHT * total
        return carry
    lax.fori_loop(0, COMPS, solution_rows, 0)

    for d in range(1, TA):
        exchange(d).wait()
    for r in range(2):
        coarse_out[pl.ds(r, TA, stride=2), :] = rc[pl.ds(r, TA, stride=8), :]
    for p in range(2):
        for m in range(4):
            message(2 * p, m).wait_send()
            message(2 * p + 1, m).wait_send()
        for i in range(4):
            corner(p, i).wait_send()
    for i in range(4):
        corner_link(i).wait_send()


def keep(value):
    return pltpu.with_memory_space_constraint(value, pltpu.HBM)


def on_device(source, gauge_links, clover_term, null_vectors, owners):
    hbm = pl.BlockSpec(memory_space=pltpu.HBM)
    vmem = pl.BlockSpec(memory_space=pltpu.VMEM)
    dma = pltpu.SemaphoreType.DMA
    x, coarse = pl.pallas_call(
        kernel,
        out_shape=(pltpu.VMEM((FIELD, 128), F32), pltpu.VMEM((2 * TA, 128), F32)),
        in_specs=[hbm] * 5,
        out_specs=(vmem, vmem),
        scratch_shapes=[
            pltpu.VMEM((5 * FIELD + 64, 128), F32),
            pltpu.VMEM((80 * PLANE, 128), F32),
            pltpu.VMEM((144 * PLANE, 128), F32),
            pltpu.VMEM((VECS, FIELD, 128), BF16),
            pltpu.VMEM((5, 2, 96, 128), F32),
            pltpu.VMEM((5, 2, 48, 128), F32),
            pltpu.VMEM((2, 4, 24, 128), F32),
            pltpu.VMEM((176, 128), F32),
            pltpu.VMEM((176, 128), F32),
            pltpu.VMEM((5, 2, 96, 128), F32),
            pltpu.VMEM((5, 2, 48, 128), F32),
            pltpu.VMEM((2, 96, 128), F32),
            pltpu.VMEM((16 * 24, 128), F32),
            pltpu.VMEM((160, 128), F32),
            pltpu.VMEM((4, 256, 1536), BF16),
            pltpu.VMEM((2, VECS * 16, 256), F32),
            pltpu.VMEM((128, 768), BF16),
            pltpu.VMEM((128, 128), F32),
            pltpu.VMEM((128, 128), F32),
            pltpu.VMEM((1, 16), jnp.int32),
            dma((6,)), dma((4, 4)), dma((4, 4)), dma((2, 4)), dma((2, 4)),
            dma((4,)), dma((4,)), dma((TA,)), dma((TA,)),
        ],
        compiler_params=pltpu.CompilerParams(
            collective_id=0, has_side_effects=True, vmem_limit_bytes=40 * 1024 * 1024
        ),
    )(
        keep(source.reshape(FIELD, 128)),
        keep(gauge_links.reshape(72 * PLANE, 128)),
        keep(clover_term.reshape(144 * PLANE, 128)),
        keep(null_vectors.reshape(VECS, FIELD, 128)),
        keep(owners.reshape(1, 16)),
    )
    return x.reshape(source.shape), coarse[:, :4 * VECS].T


def solution(mesh):
    in_specs = (
        P(None, "gz", "ta", None),
        P(None, None, "gz", "ta", None),
        P(None, None, None, None, "gz", "ta", None),
        P(None, None, "gz", "ta", None),
        P(("gz", "ta"), None),
    )
    out_specs = (P(None, "gz", "ta", None), P(None, ("gz", "ta")))
    return jax.shard_map(
        on_device, mesh=mesh, in_specs=in_specs, out_specs=out_specs, check_vma=False
    )
```
